256 devices in a mesh: dp: 16 (over y, x), ctx: 8 (over z), rank: 2 (over core).
Axes of the slice: x: 4, y: 4, z: 8, core: 2. Of those that a mesh axis runs over, the one named last changes fastest.
Arguments:
- query_rows: bfloat16 [32, 4096, 1024], P(('dp', 'rank'), 'ctx'), may hold values from -6 to 6
- key_rows: bfloat16 [32, 4096, 1024], P(('dp', 'rank'), 'ctx'), may hold values from -6 to 6
- value_rows: bfloat16 [32, 4096, 1024], P(('dp', 'rank'), 'ctx'), may hold values from -6 to 6
- gate_rows: bfloat16 [32, 4096, 1024], P(('dp', 'rank'), 'ctx'), may hold values from -6 to 6
- out_grad: bfloat16 [32, 4096, 1024], P(('dp', 'rank'), 'ctx'), may hold values from -6 to 6
- out_weight: bfloat16 [1024, 1024], P('dp'), may hold values from -0.1875 to 0.1875
- time_bias: bfloat16 [8, 128], replicated, may hold values from -3 to 3
- time_bucket: int32 [32, 4096], P(('dp', 'rank'), 'ctx'), may hold values from 0 to 127
- lengths: int32 [32, 3], P(('dp', 'rank')), may hold values from 1 to 2048, 4096 in all within a row
- band_width: int32 [32, 3], P(('dp', 'rank')), may hold values from 128 to 512, as said below
- user_grad: bfloat16 [96, 1024], P(('dp', 'rank')), may hold values from -6 to 6
- user_owner: int32 [96], replicated, may hold values from 0 to 95, each once
Outputs:
- query_grad: bfloat16 [32, 4096, 1024], P(('dp', 'rank'), 'ctx')
- key_grad: bfloat16 [32, 4096, 1024], P(('dp', 'rank'), 'ctx')
- value_grad: bfloat16 [32, 4096, 1024], P(('dp', 'rank'), 'ctx')
- gate_grad: bfloat16 [32, 4096, 1024], P(('dp', 'rank'), 'ctx')
- weight_grad: float32 [1024, 1024], P('dp')
- bias_grad: float32 [8, 128], P('ctx')
The draws below stay inside these ranges and needn't reach their ends.
Inputs may be any that keep to these rules, and one draw needn't show every extreme that they name: In every section the longest history has exactly 2048 events and the 3 lengths sum to 4096. `band_width`: in every section some user has a band of exactly 512. A permutation: ranking row r carries the gradient of encoder user user_owner[r], and encoder user g * 3 + s is user s of section g.
All inputs are finite; a program needn't handle non-finite values.
Results may differ from the reference program's by a relative error of at most 0.0059.
Values may be sent and summed in bfloat16 or wider, within the bound.
No kernel may reach another device: no remote copies, remote signals or barrier semaphores. Data moves between devices by JAX's collectives and lax.ppermute only.
A program may use at most 128 MiB of HBM per device.

```python
import math
import jax
import jax.numpy as jnp
import numpy as np
from jax import lax

HEADS = 8
HEAD_DIM = 128
NB = 128
SEQS = 3
TOK_DEV = 512
D = 1024
GROUP_EVENTS = 4096
SECTIONS = 32
USERS = 96


def draw_band_width(key, part):
    key_one, key_two = jax.random.split(jax.random.fold_in(key, 17))
    band_values = jax.random.randint(key_one, (SECTIONS, SEQS), TOK_DEV // 4, TOK_DEV + 1)
    chosen = jax.random.randint(key_two, (SECTIONS, 1), 0, SEQS)
    slot_ids = jnp.arange(SEQS)[None, :]
    return jnp.where(slot_ids == chosen, TOK_DEV, band_values).astype(jnp.int32)


def with_ends(entries, key, low, top_value):
    extent = entries.shape
    spot = [jax.random.randint(jax.random.fold_in(key, axis), (), 0, extent[axis]) for axis in range(len(extent))]
    entries = entries.at[tuple(spot)].set(low)
    longest = extent.index(max(extent))
    spot[longest] = (spot[longest] + 1) % extent[longest]
    return entries.at[tuple(spot)].set(top_value)


def block_levels(key, extent, pieces, least, high):
    def one(position, blocks):
        heights = jax.random.uniform(jax.random.fold_in(jax.random.fold_in(key, 6), position), (blocks,), jnp.float32, least / len(pieces), high / len(pieces))
        return jnp.repeat(jnp.exp(heights), extent[position] // blocks).reshape((-1,) + (1,) * (len(extent) - position - 1))

    level = one(*pieces[0])
    for cut in pieces[1:]:
        level = level * one(*cut)
    return level


def length_profile(number_of, total, reach, slope):
    weights = [(1 << 20) // math.isqrt(grade ** slope) + 1 for grade in range(2, number_of + 1)]
    rest, counts = total - reach - (number_of - 1), [1] * (number_of - 1)
    while rest > 0:
        free = [i for i in range(number_of - 1) if counts[i] < reach]
        mass, remaining = sum([weights[i] for i in free]), rest
        for i in free:
            addition = min(reach - counts[i], max(1, remaining * weights[i] // mass), rest)
            counts[i] = counts[i] + addition
            rest = rest - addition
    return np.array([reach] + counts)


def ragged_sizes(own_key, amount, total, bound, slope):
    if amount == 2:
        one = jax.random.randint(own_key, (), max(1, total - bound), min(bound, total - 1) + 1)
        return jnp.stack([one, total - one])
    tallies = jnp.asarray(length_profile(amount, total, bound, slope), jnp.int32)
    couples = (amount - 1) // 2
    giver, taker = tallies[1:1 + 2 * couples:2], tallies[2:2 + 2 * couples:2]
    slack = jnp.minimum(giver - 1, bound - taker)
    shifted = jax.random.randint(jax.random.fold_in(own_key, 1), (couples,), 0, 1 << 20) % (slack + 1)
    tallies = tallies.at[1:1 + 2 * couples:2].set(giver - shifted).at[2:2 + 2 * couples:2].set(taker + shifted)
    return tallies[jax.random.permutation(jax.random.fold_in(own_key, 2), amount)]


def noise(rng, dims, spread, bound, shards=(), kind=jnp.bfloat16):
    array = jax.random.normal(rng, dims, jnp.float32) * spread
    if len(shards) > 0:
        array = block_levels(rng, dims, shards, -0.22, 0.18) * array
    return jnp.clip(array, min=-bound, max=bound).astype(kind)


def setup_inputs(seed: int = 0) -> dict:
    key_list = jax.random.split(jax.random.key(seed), 13)
    query_rows = noise(key_list[0], (SECTIONS, GROUP_EVENTS, D), 1.0, 6.0, ((0, 32), (1, 8)))
    key_rows = noise(key_list[1], (SECTIONS, GROUP_EVENTS, D), 1.0, 6.0, ((0, 32), (1, 8)))
    value_rows = noise(key_list[2], (SECTIONS, GROUP_EVENTS, D), 1.0, 6.0, ((0, 32), (1, 8)))
    gate_rows = noise(key_list[3], (SECTIONS, GROUP_EVENTS, D), 1.0, 6.0, ((0, 32), (1, 8)))
    out_grad = noise(key_list[4], (SECTIONS, GROUP_EVENTS, D), 1.0, 6.0, ((0, 32), (1, 8)))
    out_weight = noise(key_list[5], (D, D), D ** -0.5, 0.1875, ((0, 16),))
    time_bias = noise(key_list[6], (HEADS, NB), 0.5, 3.0)
    time_bucket = with_ends(jax.random.randint(key_list[7], (SECTIONS, GROUP_EVENTS), 0, NB), jax.random.fold_in(key_list[7], 1), 0, NB - 1).astype(jnp.int32)
    lengths = jax.vmap(lambda own: ragged_sizes(own, SEQS, GROUP_EVENTS, GROUP_EVENTS // 2, 0))(jax.random.split(key_list[8], SECTIONS)).reshape((SECTIONS, SEQS)).astype(jnp.int32)
    band_width = draw_band_width(jax.random.fold_in(key_list[12], 71), 0)
    user_grad = noise(key_list[10], (USERS, D), 1.0, 6.0, ((0, 32),))
    user_owner = jax.random.permutation(key_list[11], USERS).astype(jnp.int32)
    return dict(query_rows=query_rows, key_rows=key_rows, value_rows=value_rows, gate_rows=gate_rows, out_grad=out_grad, out_weight=out_weight, time_bias=time_bias, time_bucket=time_bucket, lengths=lengths, band_width=band_width, user_grad=user_grad, user_owner=user_owner)


def owner_of(positions, user_ends):
    counted = lax.optimization_barrier(jnp.sum((positions[:, None] >= user_ends[None, :]).astype(jnp.int32), axis=1))
    return jnp.where(positions >= 0, counted, -1).astype(jnp.int32)

def band_of(owners, user_bands):
    slot_ids = jnp.arange(user_bands.shape[0], dtype=jnp.int32)
    picked = jnp.where(owners[:, None] == slot_ids[None, :], user_bands[None, :], 0)
    return lax.optimization_barrier(jnp.sum(picked, axis=1)).astype(jnp.int32)

def window_mask(query_pos, key_pos, user_ends, user_bands):
    query_owner = owner_of(query_pos, user_ends)
    key_owner = owner_of(key_pos, user_ends)
    query_band = band_of(query_owner, user_bands)
    gap_rows = query_pos[:, None] - key_pos[None, :]
    return (query_owner[:, None] == key_owner[None, :]) & (gap_rows >= 0) & (gap_rows < query_band[:, None])

def silu_slope(score_blk):
    sigmoid_val = jax.nn.sigmoid(score_blk)
    return sigmoid_val * (1.0 + score_blk * (1.0 - sigmoid_val))

def reference(query_rows, key_rows, value_rows, gate_rows, out_grad, out_weight, time_bias, time_bucket, lengths, band_width, user_grad, user_owner):
    block_rows = min(512, TOK_DEV)
    lead_rows = TOK_DEV
    window = lead_rows + block_rows
    score_scale = 1.0 / HEAD_DIM ** 0.5
    starts = jnp.arange(GROUP_EVENTS // block_rows, dtype=jnp.int32) * block_rows
    row_order = jnp.zeros((USERS,), jnp.int32).at[user_owner].set(jnp.arange(USERS, dtype=jnp.int32))
    owned_grad = user_grad[row_order].reshape(SECTIONS, SEQS, D)
    bias_table = time_bias.astype(jnp.float32)

    def one_section(totals, inputs):
        weight_sum, bias_sum = totals
        queries, keys_in, values_in, gate_vals, cotangent, buckets, hist_lengths, user_bands, user_rows = inputs
        user_ends = jnp.cumsum(hist_lengths).astype(jnp.int32)
        pad_rows = jnp.zeros((lead_rows, D), jnp.bfloat16)
        key_buf = jnp.concatenate([pad_rows, keys_in], axis=0)
        value_buf = jnp.concatenate([pad_rows, values_in], axis=0)
        bucket_buf = jnp.concatenate([jnp.zeros((lead_rows,), jnp.int32), buckets])

        def context(block_start):
            query_pos = block_start + jnp.arange(block_rows, dtype=jnp.int32)
            key_pos = block_start - lead_rows + jnp.arange(window, dtype=jnp.int32)
            valid_mask = window_mask(query_pos, key_pos, user_ends, user_bands)
            query_bucket = lax.dynamic_slice_in_dim(buckets, block_start, block_rows)
            key_bucket = lax.dynamic_slice_in_dim(bucket_buf, block_start, window)
            bucket_index = jnp.abs(query_bucket[:, None] - key_bucket[None, :]).astype(jnp.int32)
            return (valid_mask, bucket_index)

        def scores_of(head_index, block_start, head_queries, head_keys):
            valid_mask, bucket_index = context(block_start)
            query_blk = lax.dynamic_slice_in_dim(head_queries, block_start, block_rows)
            key_win = lax.dynamic_slice_in_dim(head_keys, block_start, window)
            score_blk = jnp.dot(query_blk, key_win.T, preferred_element_type=jnp.float32) * score_scale + bias_table[head_index][bucket_index]
            return (valid_mask, bucket_index, query_blk, key_win, score_blk)
        outputs = []
        for head_index in range(HEADS):
            col_lo = head_index * HEAD_DIM
            head_queries = queries[:, col_lo:col_lo + HEAD_DIM]
            head_keys = key_buf[:, col_lo:col_lo + HEAD_DIM]
            head_values = value_buf[:, col_lo:col_lo + HEAD_DIM]

            def forward_block(block_start):
                valid_mask, bucket_index, query_blk, key_win, score_blk = scores_of(head_index, block_start, head_queries, head_keys)
                value_win = lax.dynamic_slice_in_dim(head_values, block_start, window)
                attn_blk = jnp.where(valid_mask, jax.nn.silu(score_blk), 0.0).astype(jnp.bfloat16)
                return jnp.dot(attn_blk, value_win, preferred_element_type=jnp.float32)
            out_blk = lax.map(forward_block, starts)
            outputs.append(out_blk.reshape(GROUP_EVENTS, HEAD_DIM).astype(jnp.bfloat16))
        mixed_rows = jnp.concatenate(outputs, axis=1)
        total_grad = cotangent.astype(jnp.float32).at[user_ends - 1].add(user_rows.astype(jnp.float32)).astype(jnp.bfloat16)
        lifted = jnp.dot(total_grad, out_weight.T, preferred_element_type=jnp.float32)
        mixed_f = mixed_rows.astype(jnp.float32)
        center = lax.optimization_barrier(jnp.mean(mixed_f, axis=1, keepdims=True))
        deviation = mixed_f - center
        variance = lax.optimization_barrier(jnp.mean(deviation * deviation, axis=1, keepdims=True))
        inv_std = lax.rsqrt(variance + 1e-05)
        normed = deviation * inv_std
        gate_f = gate_vals.astype(jnp.float32)
        gate_grad = (lifted * normed).astype(jnp.bfloat16)
        gated_rows = (normed * gate_f).astype(jnp.bfloat16)
        weight_sum = weight_sum + jnp.dot(gated_rows.T, total_grad, preferred_element_type=jnp.float32)
        normed_grad = lifted * gate_f
        mixed_grad = (inv_std * (normed_grad - lax.optimization_barrier(jnp.mean(normed_grad, axis=1, keepdims=True)) - normed * lax.optimization_barrier(jnp.mean(normed_grad * normed, axis=1, keepdims=True)))).astype(jnp.bfloat16)
        query_parts, key_parts, value_parts, bias_parts = ([], [], [], [])
        for head_index in range(HEADS):
            col_lo = head_index * HEAD_DIM
            head_queries = queries[:, col_lo:col_lo + HEAD_DIM]
            head_keys = key_buf[:, col_lo:col_lo + HEAD_DIM]
            head_values = value_buf[:, col_lo:col_lo + HEAD_DIM]
            head_grads = mixed_grad[:, col_lo:col_lo + HEAD_DIM]

            def backward_block(carried, block_start):
                key_acc, value_acc, bias_acc = carried
                valid_mask, bucket_index, query_blk, key_win, score_blk = scores_of(head_index, block_start, head_queries, head_keys)
                value_win = lax.dynamic_slice_in_dim(head_values, block_start, window)
                grad_blk = lax.dynamic_slice_in_dim(head_grads, block_start, block_rows)
                attn_blk = jnp.where(valid_mask, jax.nn.silu(score_blk), 0.0).astype(jnp.bfloat16)
                value_part = jnp.dot(attn_blk.T, grad_blk, preferred_element_type=jnp.float32)
                attn_grad = jnp.dot(grad_blk, value_win.T, preferred_element_type=jnp.float32)
                score_grad = jnp.where(valid_mask, attn_grad * silu_slope(score_blk), 0.0).astype(jnp.bfloat16)
                query_part = jnp.dot(score_grad, key_win, preferred_element_type=jnp.float32)
                key_part = jnp.dot(score_grad.T, query_blk, preferred_element_type=jnp.float32)
                bias_acc = bias_acc + jax.ops.segment_sum(score_grad.astype(jnp.float32).reshape(-1), bucket_index.reshape(-1), num_segments=NB)
                key_acc = lax.dynamic_update_slice_in_dim(key_acc, lax.dynamic_slice_in_dim(key_acc, block_start, window) + key_part, block_start, 0)
                value_acc = lax.dynamic_update_slice_in_dim(value_acc, lax.dynamic_slice_in_dim(value_acc, block_start, window) + value_part, block_start, 0)
                return ((key_acc, value_acc, bias_acc), query_part)
            start_state = (jnp.zeros((lead_rows + GROUP_EVENTS, HEAD_DIM), jnp.float32), jnp.zeros((lead_rows + GROUP_EVENTS, HEAD_DIM), jnp.float32), jnp.zeros((NB,), jnp.float32))
            (key_acc, value_acc, bias_acc), query_blocks = lax.scan(backward_block, start_state, starts)
            query_parts.append((query_blocks.reshape(GROUP_EVENTS, HEAD_DIM) * score_scale).astype(jnp.bfloat16))
            key_parts.append((key_acc[lead_rows:] * score_scale).astype(jnp.bfloat16))
            value_parts.append(value_acc[lead_rows:].astype(jnp.bfloat16))
            bias_parts.append(bias_acc)
        bias_sum = bias_sum + jnp.stack(bias_parts, axis=0)
        results = (jnp.concatenate(query_parts, axis=1), jnp.concatenate(key_parts, axis=1), jnp.concatenate(value_parts, axis=1), gate_grad)
        return ((weight_sum, bias_sum), results)
    start_totals = (jnp.zeros((D, D), jnp.float32), jnp.zeros((HEADS, NB), jnp.float32))
    section_inputs = (query_rows, key_rows, value_rows, gate_rows, out_grad, time_bucket, lengths, band_width, owned_grad)
    (weight_grad, bias_grad), results = lax.scan(one_section, start_totals, section_inputs)
    return (results[0], results[1], results[2], results[3], weight_grad, bias_grad)
```

```python
import functools
import math

import jax
import jax.numpy as jnp
from jax import lax
from jax.experimental import pallas as pl
from jax.experimental.pallas import tpu as pltpu
from jax.sharding import PartitionSpec as P

F32 = jnp.float32
BF16 = jnp.bfloat16
HEADS = 8
DIM = 128
TOK = 512
HALF = 256
WIDTH = 1024
PAD = 16
MASKED = -1e9
SCALE = 1.0 / math.sqrt(DIM)
VMEM_LIMIT = 48 * 1024 * 1024


def dot_nt(a, b):
    return lax.dot_general(a, b, (((1,), (1,)), ((), ())), preferred_element_type=F32)


def dot_nn(a, b):
    return lax.dot_general(a, b, (((1,), (0,)), ((), ())), preferred_element_type=F32)


def dot_tn(a, b):
    return lax.dot_general(a, b, (((0,), (0,)), ((), ())), preferred_element_type=F32)


def lowest_key(meta, first, rows):
    pos = first + lax.broadcasted_iota(jnp.int32, (rows, 1), 0)
    e0, e1, e2 = meta[0], meta[1], meta[2]
    start = jnp.where(pos >= e0, e0, 0)
    band = jnp.where(pos >= e0, meta[4], meta[3])
    start = jnp.where(pos >= e1, e1, start)
    band = jnp.where(pos >= e1, meta[5], band)
    start = jnp.where(pos >= e2, e2, start)
    band = jnp.where(pos >= e2, 0, band)
    return pos, jnp.maximum(start, pos - band + 1)


def mask_tile(meta, q_first, rows, k_first, cols, causal):
    pos, low = lowest_key(meta, q_first, rows)
    key = k_first + lax.broadcasted_iota(jnp.int32, (rows, cols), 1)
    ok = key >= low
    if causal:
        ok = ok & (key <= pos)
    return jnp.where(ok, 0.0, MASKED)


def bucket_cols(row):
    count = row.shape[1]
    return jnp.transpose(jnp.broadcast_to(row.astype(F32), (DIM, count))).astype(jnp.int32)


def lanes(rows):
    return lax.broadcasted_iota(jnp.int32, (rows, DIM), 1)


def one_hot(row):
    cols = bucket_cols(row)
    return jnp.where(cols == lanes(cols.shape[0]), 1.0, 0.0).astype(BF16)


def bias_rows(table_row, cols):
    gap = jnp.abs(cols - lanes(cols.shape[0]))
    spread = jnp.broadcast_to(table_row, gap.shape)
    return jnp.take_along_axis(spread, gap, axis=1).astype(BF16)


def bias_sum(mid, cols):
    lane = lanes(cols.shape[0])
    up, down = cols + lane, cols - lane
    above = jnp.take_along_axis(mid, up & (DIM - 1), axis=1)
    below = jnp.take_along_axis(mid, down & (DIM - 1), axis=1)
    both = jnp.where(up < DIM, above, 0.0) + jnp.where((down >= 0) & (lane > 0), below, 0.0)
    return jnp.sum(both, axis=0, keepdims=True) * 0.5


def attn_of(q_aug, k_aug, mask):
    half_score = dot_nt(q_aug, k_aug) * (0.5 * SCALE) + mask
    t = jnp.tanh(half_score)
    u = 1.0 + t
    return half_score * u, t, u


def back_of(q_aug, k_aug, mask, grad, value):
    attn, t, u = attn_of(q_aug, k_aug, mask)
    slope2 = u + attn * (1.0 - t)
    score_grad2 = (dot_nt(grad, value) * slope2).astype(BF16)
    return attn.astype(BF16), score_grad2


def cat(*parts):
    return jnp.concatenate(parts, axis=1)


def own_forward_body(meta, q, k, v, bkt, tab, out, mask, hot, cols):
    h = pl.program_id(0)

    @pl.when(h == 0)
    def _():
        mask[...] = mask_tile(meta, meta[6], TOK, meta[6], TOK, True)
        hot[...] = one_hot(bkt[...])
        cols[...] = bucket_cols(bkt[...])

    q_aug = cat(q[...], bias_rows(tab[pl.ds(h, 1), :], cols[...]))
    k_aug = cat(k[...], hot[...])
    for i in range(2):
        lo, hi = i * HALF, (i + 1) * HALF
        attn, _, _ = attn_of(q_aug[lo:hi], k_aug[:hi], mask[lo:hi, :hi])
        out[lo:hi, :] = dot_nn(attn.astype(BF16), v[:hi, :])


def sent_forward_body(meta, q, q_bkt, k, v, bkt, tab, out, mask, hot, cols):
    h = pl.program_id(0)

    @pl.when(h == 0)
    def _():
        mask[...] = mask_tile(meta, meta[6] + TOK, HALF, meta[6], TOK, False)
        hot[...] = one_hot(bkt[...])
        cols[...] = bucket_cols(q_bkt[0:1, :HALF])

    q_aug = cat(q[...], bias_rows(tab[pl.ds(h, 1), :], cols[...]))
    k_aug = cat(k[...], hot[...])
    attn, _, _ = attn_of(q_aug, k_aug, mask[...])
    out[...] = dot_nn(attn.astype(BF16), v[...]).astype(BF16)


def norm_rows(mixed, lifted, gate):
    mixed = mixed.astype(BF16).astype(F32)
    center = jnp.mean(mixed, axis=1, keepdims=True)
    deviation = mixed - center
    variance = jnp.mean(deviation * deviation, axis=1, keepdims=True)
    inv_std = lax.rsqrt(variance + 1e-05)
    normed = deviation * inv_std
    gate = gate.astype(F32)
    normed_grad = lifted * gate
    mean_one = jnp.mean(normed_grad, axis=1, keepdims=True)
    mean_two = jnp.mean(normed_grad * normed, axis=1, keepdims=True)
    mixed_grad = inv_std * (normed_grad - mean_one - normed * mean_two)
    return (lifted * normed).astype(BF16), (normed * gate).astype(BF16), mixed_grad.astype(BF16)


def late_rows_body(
    meta, q, k, v, k_bkt, bkt, tab, partial, lifted, gate,
    gate_grad, gated, mixed_grad, mixed, mask, hot, cols,
):
    h = pl.program_id(0)

    @pl.when(h == 0)
    def _():
        mask[...] = mask_tile(meta, meta[6] + HALF, HALF, meta[6] - HALF, HALF, False)
        hot[...] = one_hot(k_bkt[0:1, HALF:])
        cols[...] = bucket_cols(bkt[:, HALF:])

    q_aug = cat(q[...], bias_rows(tab[pl.ds(h, 1), :], cols[...]))
    k_aug = cat(k[...], hot[...])
    attn, _, _ = attn_of(q_aug, k_aug, mask[...])
    mixed[:, pl.ds(pl.multiple_of(h * DIM, DIM), DIM)] = partial[...] + dot_nn(attn.astype(BF16), v[...])

    @pl.when(h == HEADS - 1)
    def _():
        @pl.loop(0, HALF // 32)
        def _(c):
            rows = pl.ds(pl.multiple_of(c * 32, 32), 32)
            a, b, d = norm_rows(mixed[rows, :], lifted[rows, :], gate[rows, :])
            gate_grad[rows, :] = a
            gated[rows, :] = b
            mixed_grad[rows, :] = d


def early_rows_body(partial, came, lifted, gate, _, gate_grad, gated, mixed_grad):
    for c in range(2):
        rows = slice(c * 32, c * 32 + 32)
        a, b, d = norm_rows(
            partial[rows, :] + came[rows, :].astype(F32), lifted[rows, :], gate[rows, :]
        )
        gate_grad[rows, :] = a
        gated[rows, :] = b
        mixed_grad[rows, :] = d


def lifted_body(meta, cot, users, owner, weight, lifted, total):
    @pl.when(pl.program_id(0) == 0)
    def _():
        count = users.shape[0]
        slot = lax.broadcasted_iota(jnp.int32, (DIM, count), 0)
        pick = (owner[...] == meta[7] * 3 + slot) & (slot < 3)
        rows = dot_nn(jnp.where(pick, 1.0, 0.0).astype(BF16), users[...]).astype(BF16)
        pos = meta[6] + lax.broadcasted_iota(jnp.int32, (TOK, 1), 0)
        lane = lanes(TOK)
        last = jnp.where(lane == 0, meta[0], jnp.where(lane == 1, meta[1], meta[2])) - 1
        hits = jnp.where((pos == last) & (lane < 3), 1.0, 0.0).astype(BF16)
        total[...] = (cot[...].astype(F32) + dot_nn(hits, rows)).astype(BF16)

    lifted[...] = dot_nt(total[...], weight[...])


def weight_body(meta, late, early, total, keep, send):
    part = dot_tn(early[...], total[:HALF, :]) + dot_tn(late[...], total[HALF:, :])
    part = part.reshape(4, 2, 32, WIDTH)

    @pl.when(meta[8] == 0)
    def _():
        keep[...] = part[:, 0]
        send[...] = part[:, 1].astype(BF16)

    @pl.when(meta[8] == 1)
    def _():
        keep[...] = part[:, 1]
        send[...] = part[:, 0].astype(BF16)


def own_backward_body(
    meta, q, k, v, kh, vh, kh_bkt, bkt, tab, grad_early, grad_late,
    dq, dq_early, dk, dv, bias, mask, mask_h, hot, hot_h, cols,
):
    h = pl.program_id(0)

    @pl.when(h == 0)
    def _():
        mask[...] = mask_tile(meta, meta[6], TOK, meta[6], TOK, True)
        mask_h[...] = mask_tile(meta, meta[6] + HALF, HALF, meta[6] - HALF, HALF, False)
        hot[...] = one_hot(bkt[...])
        hot_h[...] = one_hot(kh_bkt[0:1, HALF:])
        cols[...] = bucket_cols(bkt[...])

    q_aug = cat(q[...], bias_rows(tab[pl.ds(h, 1), :], cols[...]))
    k_aug = cat(k[...], hot[...])
    kh_aug = cat(kh[...], hot_h[...])
    ge, gl = grad_early[...], grad_late[...]
    attn, sg = back_of(q_aug[:HALF], k_aug[:HALF], mask[:HALF, :HALF], ge, v[:HALF, :])
    early = dot_nn(sg, k_aug[:HALF])
    dk[:HALF, :] = dot_tn(sg, q[:HALF, :])
    dv[:HALF, :] = dot_tn(attn, ge)
    attn, sg = back_of(q_aug[HALF:], k_aug, mask[HALF:, :], gl, v[...])
    late = dot_nn(sg, k_aug)
    more_k = dot_tn(sg, q[HALF:, :])
    more_v = dot_tn(attn, gl)
    dk[:HALF, :] += more_k[:HALF]
    dv[:HALF, :] += more_v[:HALF]
    dk[HALF:, :] = more_k[HALF:]
    dv[HALF:, :] = more_v[HALF:]
    _, sg = back_of(q_aug[HALF:], kh_aug, mask_h[...], gl, vh[...])
    late = late + dot_nn(sg, kh_aug)
    dq_early[...] = early[:, :DIM]
    dq[:HALF, :] = (early[:, :DIM] * (0.5 * SCALE)).astype(BF16)
    dq[HALF:, :] = (late[:, :DIM] * (0.5 * SCALE)).astype(BF16)
    bias[pl.ds(h, 1), :] = bias_sum(early[:, DIM:], cols[:HALF, :]) + bias_sum(late[:, DIM:], cols[HALF:, :])


def sent_backward_body(
    meta, qe, q_bkt, ql, grad_early, grad_late, k, v, bkt, tab, dk_own, dv_own, bias_own,
    dk, dv, dq, bias, mask, mask_l, hot, cols,
):
    h = pl.program_id(0)

    @pl.when(h == 0)
    def _():
        mask[...] = mask_tile(meta, meta[6] + TOK, HALF, meta[6], TOK, False)
        mask_l[...] = mask_tile(meta, meta[6] + TOK + HALF, HALF, meta[6] + HALF, HALF, False)
        hot[...] = one_hot(bkt[...])
        cols[...] = bucket_cols(q_bkt[0:1, :TOK])

    row = tab[pl.ds(h, 1), :]
    added = bias_rows(row, cols[...])
    k_aug = cat(k[...], hot[...])
    ge, gl = grad_early[...], grad_late[...]
    attn, sg = back_of(cat(qe[...], added[:HALF]), k_aug, mask[...], ge, v[...])
    early = dot_nn(sg, k_aug)
    dq[...] = (early[:, :DIM] * 0.5).astype(BF16)
    bias[pl.ds(h, 1), :] = bias_own[pl.ds(h, 1), :] + bias_sum(early[:, DIM:], cols[:HALF, :])
    sum_k = dk_own[...] + dot_tn(sg, qe[...])
    sum_v = dv_own[...] + dot_tn(attn, ge)
    attn, sg = back_of(cat(ql[...], added[HALF:]), k_aug[HALF:], mask_l[...], gl, v[HALF:, :])
    dk[:HALF, :] = (sum_k[:HALF] * (0.5 * SCALE)).astype(BF16)
    dv[:HALF, :] = sum_v[:HALF].astype(BF16)
    dk[HALF:, :] = ((sum_k[HALF:] + dot_tn(sg, ql[...])) * (0.5 * SCALE)).astype(BF16)
    dv[HALF:, :] = (sum_v[HALF:] + dot_tn(attn, gl)).astype(BF16)


def finish_body(own, came, _, out):
    out[...] = ((own[...] * 0.5 + came[...].astype(F32)) * SCALE).astype(BF16)


SMEM = pl.BlockSpec(memory_space=pltpu.SMEM)


def heads_of(rows, at=0):
    return pl.BlockSpec((rows, DIM), lambda h: (at, h))


def whole(*shape):
    return pl.BlockSpec(shape, lambda h: (0,) * len(shape))


def tail_rows(at, cols):
    return pl.BlockSpec((PAD, cols), lambda h: (at, 0))


def shape_of(rows, kind, cols=WIDTH):
    return jax.ShapeDtypeStruct((rows, cols), kind)


def call(body, name, grid, in_specs, out_specs, out_shape, scratch=(), aliases=None, flops=0, moved=0):
    return pl.pallas_call(
        body,
        name=name,
        grid=grid,
        in_specs=in_specs,
        out_specs=out_specs,
        out_shape=out_shape,
        scratch_shapes=list(scratch),
        input_output_aliases=aliases or {},
        cost_estimate=pl.CostEstimate(flops=flops, bytes_accessed=moved, transcendentals=0),
        compiler_params=pltpu.CompilerParams(vmem_limit_bytes=VMEM_LIMIT),
    )


def on_device(
    query_rows, key_rows, value_rows, gate_rows, out_grad, out_weight,
    time_bias, time_bucket, lengths, band_width, user_grad, user_owner,
):
    q, k, v = query_rows[0], key_rows[0], value_rows[0]
    gate, cot = gate_rows[0], out_grad[0]
    bkt = time_bucket
    ctx = lax.axis_index("ctx")
    rank = lax.axis_index("rank")
    n_ctx = lax.axis_size("ctx")
    n_dp = lax.axis_size("dp")
    section = lax.axis_index("dp") * lax.axis_size("rank") + rank
    ends = jnp.cumsum(lengths[0])
    first = ctx * TOK
    meta = jnp.concatenate(
        [ends, band_width[0], jnp.stack([first, section, rank])]
    ).astype(jnp.int32)
    tab = time_bias.astype(F32) * math.sqrt(DIM)
    up = [(i, i + 1) for i in range(n_ctx - 1)]
    down = [(i + 1, i) for i in range(n_ctx - 1)]

    bkt_rows = jnp.pad(
        jnp.broadcast_to(bkt.astype(BF16), (PAD, TOK)), ((0, 0), (0, WIDTH - TOK))
    )
    q_early = lax.ppermute(jnp.concatenate([q[:HALF], bkt_rows]), "ctx", down)
    kv_came = lax.ppermute(jnp.concatenate([k[HALF:], v[HALF:], bkt_rows]), "ctx", up)
    q_late = lax.ppermute(q[HALF:], "ctx", down)
    users = lax.all_to_all(
        jnp.broadcast_to(user_grad[None], (2 * n_dp,) + user_grad.shape), ("dp", "rank"), 0, 0, tiled=True
    ).reshape(-1, WIDTH)
    weight = lax.all_to_all(
        jnp.broadcast_to(out_weight[None], (n_dp,) + out_weight.shape), "dp", 0, 0, tiled=True
    ).reshape(WIDTH, WIDTH)

    col = pltpu.VMEM((TOK, DIM), jnp.int32)
    half_col = pltpu.VMEM((HALF, DIM), jnp.int32)
    hot = pltpu.VMEM((TOK, DIM), BF16)
    half_hot = pltpu.VMEM((HALF, DIM), BF16)

    own_out = call(
        own_forward_body, "own_forward", (HEADS,),
        [SMEM, heads_of(TOK), heads_of(TOK), heads_of(TOK), whole(1, TOK), whole(HEADS, DIM)],
        heads_of(TOK), shape_of(TOK, F32),
        [pltpu.VMEM((TOK, TOK), F32), hot, col],
        flops=4_000_000_000, moved=5 << 20,
    )(meta, q, k, v, bkt, tab)

    lifted, total = call(
        lifted_body, "lifted", (4,),
        [SMEM, whole(TOK, WIDTH), whole(users.shape[0], WIDTH), whole(1, users.shape[0]),
         pl.BlockSpec((HALF, WIDTH), lambda h: (h, 0))],
        (pl.BlockSpec((TOK, HALF), lambda h: (0, h)), whole(TOK, WIDTH)),
        (shape_of(TOK, F32), shape_of(TOK, BF16)),
        flops=1_200_000_000, moved=6 << 20,
    )(meta, cot, users, user_owner[None, :], weight)

    sent_out = call(
        sent_forward_body, "sent_forward", (HEADS,),
        [SMEM, heads_of(HALF), tail_rows(HALF // PAD, TOK), heads_of(TOK), heads_of(TOK),
         whole(1, TOK), whole(HEADS, DIM)],
        heads_of(HALF), shape_of(HALF, BF16),
        [pltpu.VMEM((HALF, TOK), F32), hot, half_col],
        flops=2_000_000_000, moved=3 << 20,
    )(meta, q_early, q_early, k, v, bkt, tab)
    out_came = lax.ppermute(sent_out, "ctx", up)

    late_half = pl.BlockSpec((HALF, WIDTH), lambda h: (1, 0))
    gate_grad, gated_late, grad_late = call(
        late_rows_body, "late_rows", (HEADS,),
        [SMEM, heads_of(HALF, 1), heads_of(HALF, 0), heads_of(HALF, 1), tail_rows(TOK // PAD, TOK),
         whole(1, TOK), whole(HEADS, DIM), heads_of(HALF, 1), late_half, late_half],
        (late_half, whole(HALF, WIDTH), whole(HALF, WIDTH)),
        (shape_of(TOK, BF16), shape_of(HALF, BF16), shape_of(HALF, BF16)),
        [pltpu.VMEM((HALF, WIDTH), F32), pltpu.VMEM((HALF, HALF), F32), half_hot, half_col],
        flops=1_000_000_000, moved=7 << 20,
    )(meta, q, kv_came, kv_came, kv_came, bkt, tab, own_out, lifted, gate)
    grad_late_came = lax.ppermute(grad_late, "ctx", down)

    part = pl.BlockSpec((64, WIDTH), lambda h: (h, 0))
    gate_grad, gated_early, grad_early = call(
        early_rows_body, "early_rows", (HALF // 64,),
        [part, part, part, part, pl.BlockSpec(memory_space=pl.ANY)],
        (part, part, part),
        (shape_of(TOK, BF16), shape_of(HALF, BF16), shape_of(HALF, BF16)),
        aliases={4: 0}, flops=10_000_000, moved=5 << 20,
    )(own_out, out_came, lifted, gate, gate_grad)
    grad_early_came = lax.ppermute(grad_early, "ctx", down)

    cut = pl.BlockSpec((HALF, HALF), lambda h: (0, h))
    piece = pl.BlockSpec((4, 32, WIDTH), lambda h: (h, 0, 0))
    keep, send = call(
        weight_body, "weight_part", (4,),
        [SMEM, cut, cut, whole(TOK, WIDTH)],
        (piece, piece),
        (jax.ShapeDtypeStruct((16, 32, WIDTH), F32), jax.ShapeDtypeStruct((16, 32, WIDTH), BF16)),
        flops=1_100_000_000, moved=6 << 20,
    )(meta, gated_late, gated_early, total)
    other = lax.ppermute(send, "rank", [(0, 1), (1, 0)])
    pair = (keep + other.astype(F32)).astype(BF16)
    rows = jnp.sum(lax.all_to_all(pair, "dp", 0, 0, tiled=True).astype(F32), axis=0).astype(BF16)
    rows = lax.all_to_all(
        jnp.broadcast_to(rows[None], (2 * n_ctx,) + rows.shape), ("ctx", "rank"), 0, 0, tiled=True
    )
    weight_grad = jnp.sum(
        rows.reshape(n_ctx, 64, WIDTH).astype(F32), axis=0
    )

    dq, dq_early, dk_own, dv_own, bias_own = call(
        own_backward_body, "own_backward", (HEADS,),
        [SMEM, heads_of(TOK), heads_of(TOK), heads_of(TOK), heads_of(HALF, 0), heads_of(HALF, 1),
         tail_rows(TOK // PAD, TOK), whole(1, TOK), whole(HEADS, DIM), heads_of(HALF), heads_of(HALF)],
        (heads_of(TOK), heads_of(HALF), heads_of(TOK), heads_of(TOK), whole(HEADS, DIM)),
        (shape_of(TOK, BF16), shape_of(HALF, F32), shape_of(TOK, F32), shape_of(TOK, F32),
         shape_of(HEADS, F32, DIM)),
        [pltpu.VMEM((TOK, TOK), F32), pltpu.VMEM((HALF, HALF), F32), hot, half_hot, col],
        flops=8_000_000_000, moved=12 << 20,
    )(meta, q, k, v, kv_came, kv_came, kv_came, bkt, tab, grad_early, grad_late)

    dk, dv, dq_sent, bias = call(
        sent_backward_body, "sent_backward", (HEADS,),
        [SMEM, heads_of(HALF), tail_rows(HALF // PAD, WIDTH), heads_of(HALF), heads_of(HALF),
         heads_of(HALF), heads_of(TOK), heads_of(TOK), whole(1, TOK), whole(HEADS, DIM),
         heads_of(TOK), heads_of(TOK), whole(HEADS, DIM)],
        (heads_of(TOK), heads_of(TOK), heads_of(HALF), whole(HEADS, DIM)),
        (shape_of(TOK, BF16), shape_of(TOK, BF16), shape_of(HALF, BF16), shape_of(HEADS, F32, DIM)),
        [pltpu.VMEM((HALF, TOK), F32), pltpu.VMEM((HALF, HALF), F32), hot, col],
        flops=5_000_000_000, moved=10 << 20,
    )(meta, q_early, q_early, q_late, grad_early_came, grad_late_came, k, v, bkt, tab,
      dk_own, dv_own, bias_own)
    dq_came = lax.ppermute(dq_sent, "ctx", up)

    dq = call(
        finish_body, "finish", (HALF // 64,),
        [part, part, pl.BlockSpec(memory_space=pl.ANY)],
        part, shape_of(TOK, BF16), aliases={2: 0}, flops=1_000_000, moved=2 << 20,
    )(dq_early, dq_came, dq)

    spread = jnp.broadcast_to(bias[None, :, None], (n_dp, n_ctx, 2, DIM)).reshape(-1, DIM)
    bias_grad = jnp.sum(
        lax.all_to_all(spread, ("dp", "ctx", "rank"), 0, 0, tiled=True), axis=0, keepdims=True
    )
    return (dq[None], dk[None], dv[None], gate_grad[None], weight_grad, bias_grad)


def solution(mesh):
    rows = P(("dp", "rank"), "ctx", None)
    users = P(("dp", "rank"), None)
    return jax.shard_map(
        on_device,
        mesh=mesh,
        in_specs=(
            rows, rows, rows, rows, rows, P("dp", None), P(), P(("dp", "rank"), "ctx"),
            users, users, users, P(),
        ),
        out_specs=(rows, rows, rows, rows, P("dp", None), P("ctx", None)),
        check_vma=False,
    )
```

```python
import functools
import math

import jax
import jax.numpy as jnp
from jax import lax
from jax.experimental import pallas as pl
from jax.experimental.pallas import tpu as pltpu
from jax.sharding import PartitionSpec as P

F32 = jnp.float32
BF16 = jnp.bfloat16
HEADS = 8
DIM = 128
TOK = 512
HALF = 256
WIDTH = 1024
MASKED = -1e9
SCALE = 1.0 / math.sqrt(DIM)
STEP = 2
COST = 1
VMEM_LIMIT = 60 * 1024 * 1024


def dot_nt(a, b):
    return lax.dot_general(a, b, (((1,), (1,)), ((), ())), preferred_element_type=F32)


def dot_nn(a, b):
    return lax.dot_general(a, b, (((1,), (0,)), ((), ())), preferred_element_type=F32)


def dot_tn(a, b):
    return lax.dot_general(a, b, (((0,), (0,)), ((), ())), preferred_element_type=F32)


def lowest_key(meta, first, rows):
    pos = first + lax.broadcasted_iota(jnp.int32, (rows, 1), 0)
    e0, e1, e2 = meta[0], meta[1], meta[2]
    start = jnp.where(pos >= e0, e0, 0)
    band = jnp.where(pos >= e0, meta[4], meta[3])
    start = jnp.where(pos >= e1, e1, start)
    band = jnp.where(pos >= e1, meta[5], band)
    start = jnp.where(pos >= e2, e2, start)
    band = jnp.where(pos >= e2, 0, band)
    return pos, jnp.maximum(start, pos - band + 1)


def mask_tile(meta, q_first, rows, k_first, cols, causal):
    pos, low = lowest_key(meta, q_first, rows)
    key = k_first + lax.broadcasted_iota(jnp.int32, (rows, cols), 1)
    ok = key >= low
    if causal:
        ok = ok & (key <= pos)
    return jnp.where(ok, 0.0, MASKED)


def bucket_cols(row):
    count = row.shape[1]
    return jnp.transpose(jnp.broadcast_to(row.astype(F32), (DIM, count))).astype(jnp.int32)


def lanes(rows):
    return lax.broadcasted_iota(jnp.int32, (rows, DIM), 1)


def one_hot(row):
    cols = bucket_cols(row)
    return jnp.where(cols == lanes(cols.shape[0]), 1.0, 0.0).astype(BF16)


def bias_rows(table_row, cols):
    gap = jnp.abs(cols - lanes(cols.shape[0]))
    spread = jnp.broadcast_to(table_row, gap.shape)
    return jnp.take_along_axis(spread, gap, axis=1).astype(BF16)


def bias_sum(mid, cols):
    lane = lanes(cols.shape[0])
    up, down = cols + lane, cols - lane
    above = jnp.take_along_axis(mid, up & (DIM - 1), axis=1)
    below = jnp.take_along_axis(mid, down & (DIM - 1), axis=1)
    both = jnp.where(up < DIM, above, 0.0) + jnp.where((down >= 0) & (lane > 0), below, 0.0)
    return jnp.sum(both, axis=0, keepdims=True) * 0.5


def attn_of(q_aug, k_aug, mask):
    half_score = dot_nt(q_aug, k_aug) * (0.5 * SCALE) + mask
    t = jnp.tanh(half_score)
    u = 1.0 + t
    return half_score * u, t, u


def back_of(q_aug, k_aug, mask, grad, value):
    attn, t, u = attn_of(q_aug, k_aug, mask)
    slope2 = u + attn * (1.0 - t)
    score_grad2 = (dot_nt(grad, value) * slope2).astype(BF16)
    return attn.astype(BF16), score_grad2


def cat(*parts):
    return jnp.concatenate(parts, axis=1)


def each_head(tab, base=0):
    for j in range(STEP):
        h = base + pl.program_id(0) * STEP + j
        yield h, slice(j * DIM, (j + 1) * DIM), tab[pl.ds(h, 1), :]


def own_forward_body(base, meta, q, k, v, bkt, tab, *rest):
    out, mask, hot, cols = rest[-4:]

    @pl.when(pl.program_id(0) == 0)
    def _():
        mask[...] = mask_tile(meta, meta[6], TOK, meta[6], TOK, True)
        hot[...] = one_hot(bkt[...])
        cols[...] = bucket_cols(bkt[...])

    for _, at, row in each_head(tab, base):
        q_aug = cat(q[:, at], bias_rows(row, cols[...]))
        k_aug = cat(k[:, at], hot[...])
        for i in range(2):
            lo, hi = i * HALF, (i + 1) * HALF
            attn, _, _ = attn_of(q_aug[lo:hi], k_aug[:hi], mask[lo:hi, :hi])
            out[lo:hi, at] = dot_nn(attn.astype(BF16), v[:hi, at])


def norm_of(mixed):
    mixed = mixed.astype(F32)
    center = jnp.mean(mixed, axis=1, keepdims=True)
    deviation = mixed - center
    variance = jnp.mean(deviation * deviation, axis=1, keepdims=True)
    inv_std = lax.rsqrt(variance + 1e-05)
    return deviation * inv_std, inv_std


def rows_body(
    meta, q, k, v, k_bkt, bkt, tab, partial, lifted, gate,
    gate_grad, gated, mixed_grad, total, mask, hot, cols,
):
    @pl.when(pl.program_id(0) == 0)
    def _():
        mask[...] = mask_tile(meta, meta[6], TOK, meta[6] - TOK, TOK, False)
        hot[...] = one_hot(k_bkt[...])
        cols[...] = bucket_cols(bkt[...])

    for h, at, row in each_head(tab):
        q_aug = cat(q[:, at], bias_rows(row, cols[...]))
        k_aug = cat(k[:, at], hot[...])
        column = pl.ds(pl.multiple_of(h * DIM, DIM), DIM)
        for i in range(2):
            lo, hi = i * HALF, (i + 1) * HALF
            attn, _, _ = attn_of(q_aug[lo:hi], k_aug[lo:], mask[lo:hi, lo:])
            total[lo:hi, column] = (
                partial[lo:hi, at] + dot_nn(attn.astype(BF16), v[lo:, at])
            ).astype(BF16)

    @pl.when(pl.program_id(0) == HEADS // STEP - 1)
    def _():
        @pl.loop(0, TOK // 64)
        def _(c):
            for i in range(2):
                rows = pl.ds(pl.multiple_of(c * 64 + i * 32, 32), 32)
                lift = lifted[rows, :]
                gate_f = gate[rows, :].astype(F32)
                normed, inv_std = norm_of(total[rows, :])
                gate_grad[rows, :] = (lift * normed).astype(BF16)
                gated[rows, :] = (normed * gate_f).astype(BF16)
                normed_grad = lift * gate_f
                mean_one = jnp.mean(normed_grad, axis=1, keepdims=True)
                mean_two = jnp.mean(normed_grad * normed, axis=1, keepdims=True)
                mixed_grad[rows, :] = (
                    inv_std * (normed_grad - mean_one - normed * mean_two)
                ).astype(BF16)


def lifted_body(meta, cot, users, owner, weight, lifted, total):
    @pl.when(pl.program_id(0) == 0)
    def _():
        count = users.shape[0]
        slot = lax.broadcasted_iota(jnp.int32, (DIM, count), 0)
        source = lax.broadcasted_iota(jnp.int32, (DIM, count), 1)
        pick = (owner[...] == meta[7] * 3 + (slot >> 3)) & ((source & 7) == (slot & 7)) & (slot < 24)
        rows = dot_nn(jnp.where(pick, 1.0, 0.0).astype(BF16), users[...]).astype(BF16)
        pos = meta[6] + lax.broadcasted_iota(jnp.int32, (TOK, 1), 0)
        lane = lanes(TOK)
        user = lane >> 3
        last = jnp.where(user == 0, meta[0], jnp.where(user == 1, meta[1], meta[2])) - 1
        hit = (pos == last) & (lane < 24)
        for c in range(WIDTH // DIM):
            at = slice(c * DIM, (c + 1) * DIM)
            hits = jnp.where(hit & ((lane & 7) == c), 1.0, 0.0).astype(BF16)
            total[:, at] = (cot[:, at].astype(F32) + dot_nn(hits, rows)).astype(BF16)

    lifted[...] = dot_nt(total[...], weight[...])


def weight_body(meta, gated, total, keep, send):
    part = dot_tn(gated[...], total[...])
    part = part.reshape(4, 2, 32, WIDTH)

    @pl.when(meta[8] == 0)
    def _():
        keep[...] = part[:, 0]
        send[...] = part[:, 1].astype(BF16)

    @pl.when(meta[8] == 1)
    def _():
        keep[...] = part[:, 1]
        send[...] = part[:, 0].astype(BF16)


def own_backward_body(
    meta, q, k, v, kh, vh, kh_bkt, bkt, tab, grad,
    dq, dk, dv, bias, mask, mask_h, hot, hot_h, cols,
):
    @pl.when(pl.program_id(0) == 0)
    def _():
        mask[...] = mask_tile(meta, meta[6], TOK, meta[6], TOK, True)
        mask_h[...] = mask_tile(meta, meta[6], TOK, meta[6] - TOK, TOK, False)
        hot[...] = one_hot(bkt[...])
        hot_h[...] = one_hot(kh_bkt[...])
        cols[...] = bucket_cols(bkt[...])

    for h, at, row in each_head(tab):
        own_backward_head(
            q[:, at], k[:, at], v[:, at], kh[:, at], vh[:, at], row, grad[:, at],
            dq, dk, dv, bias, mask, mask_h, hot, hot_h, cols, h, at,
        )


def own_backward_head(
    q, k, v, kh, vh, row, grad, dq, dk, dv, bias, mask, mask_h, hot, hot_h, cols, h, at
):
    q_aug = cat(q, bias_rows(row, cols[...]))
    k_aug = cat(k, hot[...])
    kh_aug = cat(kh, hot_h[...])
    ge, gl = grad[:HALF], grad[HALF:]
    attn, sg = back_of(q_aug[:HALF], k_aug[:HALF], mask[:HALF, :HALF], ge, v[:HALF])
    early = dot_nn(sg, k_aug[:HALF])
    dk[:HALF, at] = dot_tn(sg, q[:HALF])
    dv[:HALF, at] = dot_tn(attn, ge)
    _, sg = back_of(q_aug[:HALF], kh_aug, mask_h[:HALF, :], ge, vh)
    early = early + dot_nn(sg, kh_aug)
    attn, sg = back_of(q_aug[HALF:], k_aug, mask[HALF:, :], gl, v)
    late = dot_nn(sg, k_aug)
    more_k = dot_tn(sg, q[HALF:])
    more_v = dot_tn(attn, gl)
    dk[:HALF, at] += more_k[:HALF]
    dv[:HALF, at] += more_v[:HALF]
    dk[HALF:, at] = more_k[HALF:]
    dv[HALF:, at] = more_v[HALF:]
    _, sg = back_of(q_aug[HALF:], kh_aug[HALF:], mask_h[HALF:, HALF:], gl, vh[HALF:])
    late = late + dot_nn(sg, kh_aug[HALF:])
    dq[:HALF, at] = (early[:, :DIM] * (0.5 * SCALE)).astype(BF16)
    dq[HALF:, at] = (late[:, :DIM] * (0.5 * SCALE)).astype(BF16)
    bias[pl.ds(h, 1), :] = bias_sum(early[:, DIM:], cols[:HALF, :]) + bias_sum(late[:, DIM:], cols[HALF:, :])


def sent_backward_body(
    base, meta, qs, q_bkt, grad, k, v, bkt, tab, dk_own, dv_own, *rest
):
    dk, dv, mask, mask_l, hot, cols = rest[-6:]

    @pl.when(pl.program_id(0) == 0)
    def _():
        mask[...] = mask_tile(meta, meta[6] + TOK, HALF, meta[6], TOK, False)
        mask_l[...] = mask_tile(meta, meta[6] + TOK + HALF, HALF, meta[6] + HALF, HALF, False)
        hot[...] = one_hot(bkt[...])
        cols[...] = bucket_cols(q_bkt[...])

    for _, at, row in each_head(tab, base):
        added = bias_rows(row, cols[...])
        k_aug = cat(k[:, at], hot[...])
        ge, gl = grad[:HALF, at], grad[HALF:, at]
        qe, ql = qs[:HALF, at], qs[HALF:, at]
        attn, sg = back_of(cat(qe, added[:HALF]), k_aug, mask[...], ge, v[:, at])
        sum_k = dk_own[:, at] + dot_tn(sg, qe)
        sum_v = dv_own[:, at] + dot_tn(attn, ge)
        attn, sg = back_of(cat(ql, added[HALF:]), k_aug[HALF:], mask_l[...], gl, v[HALF:, at])
        dk[:HALF, at] = (sum_k[:HALF] * (0.5 * SCALE)).astype(BF16)
        dv[:HALF, at] = sum_v[:HALF].astype(BF16)
        dk[HALF:, at] = ((sum_k[HALF:] + dot_tn(sg, ql)) * (0.5 * SCALE)).astype(BF16)
        dv[HALF:, at] = (sum_v[HALF:] + dot_tn(attn, gl)).astype(BF16)


SMEM = pl.BlockSpec(memory_space=pltpu.SMEM)


def heads_of(rows, at=0):
    return pl.BlockSpec((rows, STEP * DIM), lambda h: (at, h))


def whole(*shape):
    return pl.BlockSpec(shape, lambda h: (0,) * len(shape))


def shape_of(rows, kind, cols=WIDTH):
    return jax.ShapeDtypeStruct((rows, cols), kind)


def call(body, name, grid, in_specs, out_specs, out_shape, scratch=(), aliases=None, flops=0, moved=0):
    return pl.pallas_call(
        body,
        name=name,
        grid=grid,
        in_specs=in_specs,
        out_specs=out_specs,
        out_shape=out_shape,
        scratch_shapes=list(scratch),
        input_output_aliases=aliases or {},
        cost_estimate=pl.CostEstimate(flops=flops // COST, bytes_accessed=moved // COST, transcendentals=0),
        compiler_params=pltpu.CompilerParams(vmem_limit_bytes=VMEM_LIMIT),
    )


def on_device(
    query_rows, key_rows, value_rows, gate_rows, out_grad, out_weight,
    time_bias, time_bucket, lengths, band_width, user_grad, user_owner,
):
    q, k, v = query_rows[0], key_rows[0], value_rows[0]
    gate, cot = gate_rows[0], out_grad[0]
    bkt = time_bucket
    ctx = lax.axis_index("ctx")
    rank = lax.axis_index("rank")
    n_ctx = lax.axis_size("ctx")
    n_dp = lax.axis_size("dp")
    section = lax.axis_index("dp") * lax.axis_size("rank") + rank
    ends = jnp.cumsum(lengths[0])
    first = ctx * TOK
    meta = jnp.concatenate(
        [ends, band_width[0], jnp.stack([first, section, rank])]
    ).astype(jnp.int32)
    tab = time_bias.astype(F32) * math.sqrt(DIM)
    up = [(i, i + 1) for i in range(n_ctx - 1)]
    down = [(i + 1, i) for i in range(n_ctx - 1)]

    k_came = lax.ppermute(k, "ctx", up)
    v_came = lax.ppermute(v, "ctx", up)
    q_came = lax.ppermute(q, "ctx", down)
    bkt_before = lax.ppermute(bkt, "ctx", up)
    bkt_after = lax.ppermute(bkt, "ctx", down)
    owner = jnp.pad(
        jnp.repeat(user_owner.reshape(-1, 3), 8, axis=1), ((0, 0), (0, 8)), constant_values=-1
    ).reshape(1, WIDTH)

    col = pltpu.VMEM((TOK, DIM), jnp.int32)
    hot = pltpu.VMEM((TOK, DIM), BF16)

    own_half = functools.partial(
        call, grid=(HEADS // STEP // 2,), out_shape=shape_of(TOK, F32),
        scratch=[pltpu.VMEM((TOK, TOK), F32), hot, col], flops=2_000_000_000, moved=3 << 20,
    )
    shift = HEADS // STEP // 2
    lower = pl.BlockSpec((TOK, STEP * DIM), lambda h: (0, h))
    upper = pl.BlockSpec((TOK, STEP * DIM), lambda h: (0, h + shift))
    own_out = own_half(
        functools.partial(own_forward_body, 0), "own_forward_low",
        in_specs=[SMEM, lower, lower, lower, whole(1, TOK), whole(HEADS, DIM)], out_specs=lower,
    )(meta, q, k, v, bkt, tab)

    pieces = jnp.pad(user_grad.reshape(24, DIM), ((0, 8), (0, 0)))
    half_weight = lax.dynamic_slice_in_dim(out_weight, rank * 32, 32)
    shared = jnp.concatenate([half_weight, pieces], axis=1)
    weight = lax.all_to_all(
        jnp.broadcast_to(shared[None], (2 * n_dp, 32, WIDTH + DIM)), ("dp", "rank"), 0, 0, tiled=True
    ).reshape(WIDTH, WIDTH + DIM)

    own_out = own_half(
        functools.partial(own_forward_body, HEADS // 2), "own_forward_high",
        in_specs=[SMEM, upper, upper, upper, whole(1, TOK), whole(HEADS, DIM),
                  pl.BlockSpec(memory_space=pl.ANY)],
        out_specs=upper, aliases={6: 0},
    )(meta, q, k, v, bkt, tab, own_out)

    lifted, total = call(
        lifted_body, "lifted", (4,),
        [SMEM, whole(TOK, WIDTH), pl.BlockSpec((WIDTH, DIM), lambda h: (0, WIDTH // DIM)),
         whole(1, WIDTH), pl.BlockSpec((HALF, WIDTH), lambda h: (h, 0))],
        (pl.BlockSpec((TOK, HALF), lambda h: (0, h)), whole(TOK, WIDTH)),
        (shape_of(TOK, F32), shape_of(TOK, BF16)),
        flops=1_200_000_000, moved=6 << 20,
    )(meta, cot, weight, owner, weight)

    meta_rows, q_came, bkt_after = lax.optimization_barrier((meta, q_came, bkt_after))
    gate_grad, gated, grad = call(
        rows_body, "rows", (HEADS // STEP,),
        [SMEM, heads_of(TOK), heads_of(TOK), heads_of(TOK), whole(1, TOK), whole(1, TOK),
         whole(HEADS, DIM), heads_of(TOK), whole(TOK, WIDTH), whole(TOK, WIDTH)],
        (whole(TOK, WIDTH),) * 3,
        (shape_of(TOK, BF16),) * 3,
        [pltpu.VMEM((TOK, WIDTH), BF16), pltpu.VMEM((TOK, TOK), F32), hot, col],
        flops=2_000_000_000, moved=10 << 20,
    )(meta_rows, q, k_came, v_came, bkt_before, bkt, tab, own_out, lifted, gate)
    grad_came = lax.ppermute(grad, "ctx", down)

    cut = pl.BlockSpec((TOK, HALF), lambda h: (0, h))
    piece = pl.BlockSpec((4, 32, WIDTH), lambda h: (h, 0, 0))
    keep, send = call(
        weight_body, "weight_part", (4,),
        [SMEM, cut, whole(TOK, WIDTH)],
        (piece, piece),
        (jax.ShapeDtypeStruct((16, 32, WIDTH), F32), jax.ShapeDtypeStruct((16, 32, WIDTH), BF16)),
        flops=1_100_000_000, moved=6 << 20,
    )(meta, gated, total)
    other = lax.ppermute(send, "rank", [(0, 1), (1, 0)])
    pair = (keep + other.astype(F32)).astype(BF16)
    rows = lax.all_to_all(pair, "dp", 0, 0, tiled=True)
    meta_own, _ = lax.optimization_barrier((meta, pair))
    passed = pl.BlockSpec(memory_space=pl.ANY)

    dq, dk_own, dv_own, bias = call(
        own_backward_body, "own_backward", (HEADS // STEP,),
        [SMEM] + [heads_of(TOK)] * 5 + [whole(1, TOK), whole(1, TOK), whole(HEADS, DIM), heads_of(TOK)],
        (heads_of(TOK), heads_of(TOK), heads_of(TOK), whole(HEADS, DIM)),
        (shape_of(TOK, BF16), shape_of(TOK, F32), shape_of(TOK, F32), shape_of(HEADS, F32, DIM)),
        [pltpu.VMEM((TOK, TOK), F32), pltpu.VMEM((TOK, TOK), F32), hot, hot, col],
        flops=10_000_000_000, moved=12 << 20,
    )(meta_own, q, k, v, k_came, v_came, bkt_before, bkt, tab, grad)

    spread = jnp.broadcast_to(bias[None, :, None], (n_dp, n_ctx, 2, DIM)).reshape(-1, DIM)
    rows, spread, grad_came = lax.optimization_barrier((rows, spread, grad_came))
    bias_all = lax.all_to_all(spread, ("dp", "ctx", "rank"), 0, 0, tiled=True)
    rows = jnp.sum(rows.astype(F32), axis=0)
    def sent_half(at, meta, *done):
        cols = functools.partial(pl.BlockSpec, index_map=lambda h: (0, h + at))
        out = cols((TOK, STEP * DIM))
        return call(
            functools.partial(sent_backward_body, at * STEP), "sent_backward", (HEADS // STEP // 2,),
            [SMEM, out, whole(1, TOK), out, out, out, whole(1, TOK), whole(HEADS, DIM), out, out]
            + [passed] * len(done),
            (out, out),
            (shape_of(TOK, BF16), shape_of(TOK, BF16)),
            [pltpu.VMEM((HALF, TOK), F32), pltpu.VMEM((HALF, HALF), F32), hot, col],
            aliases={10: 0, 11: 1} if done else None,
            flops=2_000_000_000, moved=5 << 20,
        )(meta, q_came, bkt_after, grad_came, k, v, bkt, tab, dk_own, dv_own, *done)

    def add_swap(rows, bit):
        return rows + lax.ppermute(rows, "ctx", [(i, i ^ bit) for i in range(n_ctx)])

    rows, meta_back = lax.optimization_barrier((rows, meta))
    done = sent_half(0, meta_back)
    rows = add_swap(rows, 1)
    rows, meta_back, *done = lax.optimization_barrier((rows, meta, *done))
    dk, dv = sent_half(HEADS // STEP // 2, meta_back, *done)
    rows = add_swap(rows, 2)
    rows, dk, dv = lax.optimization_barrier((rows, dk, dv))
    rows = add_swap(rows, 4)
    rows, bias_all = lax.optimization_barrier((rows, bias_all))
    other_rows = lax.ppermute(rows, "rank", [(0, 1), (1, 0)])
    weight_grad = jnp.concatenate(
        [jnp.where(rank == 0, rows, other_rows), jnp.where(rank == 0, other_rows, rows)], axis=0
    )
    bias_grad = jnp.sum(bias_all, axis=0, keepdims=True)
    return (dq[None], dk[None], dv[None], gate_grad[None], weight_grad, bias_grad)


def solution(mesh):
    rows = P(("dp", "rank"), "ctx", None)
    users = P(("dp", "rank"), None)
    return jax.shard_map(
        on_device,
        mesh=mesh,
        in_specs=(
            rows, rows, rows, rows, rows, P("dp", None), P(), P(("dp", "rank"), "ctx"),
            users, users, users, P(),
        ),
        out_specs=(rows, rows, rows, rows, P("dp", None), P("ctx", None)),
        check_vma=False,
    )
```

```python
import functools
import math

import jax
import jax.numpy as jnp
from jax import lax
from jax.experimental import pallas as pl
from jax.experimental.pallas import tpu as pltpu
from jax.sharding import PartitionSpec as P

F32 = jnp.float32
BF16 = jnp.bfloat16
HEADS = 8
DIM = 128
TOK = 512
HALF = 256
WIDTH = 1024
PAD = 16
MASKED = -1e9
SCALE = 1.0 / math.sqrt(DIM)
STEP = 2
COST = 1
VMEM_LIMIT = 60 * 1024 * 1024


def dot_nt(a, b):
    return lax.dot_general(a, b, (((1,), (1,)), ((), ())), preferred_element_type=F32)


def dot_nn(a, b):
    return lax.dot_general(a, b, (((1,), (0,)), ((), ())), preferred_element_type=F32)


def dot_tn(a, b):
    return lax.dot_general(a, b, (((0,), (0,)), ((), ())), preferred_element_type=F32)


def lowest_key(meta, first, rows, axis=0):
    shape = (rows, 1) if axis == 0 else (1, rows)
    pos = first + lax.broadcasted_iota(jnp.int32, shape, axis)
    e0, e1, e2 = meta[0], meta[1], meta[2]
    start = jnp.where(pos >= e0, e0, 0)
    band = jnp.where(pos >= e0, meta[4], meta[3])
    start = jnp.where(pos >= e1, e1, start)
    band = jnp.where(pos >= e1, meta[5], band)
    start = jnp.where(pos >= e2, e2, start)
    band = jnp.where(pos >= e2, 0, band)
    return pos, jnp.maximum(start, pos - band + 1)


def mask_tile(meta, q_first, rows, k_first, cols, causal, turned=False):
    axis = 1 if turned else 0
    pos, low = lowest_key(meta, q_first, rows, axis)
    shape = (cols, rows) if turned else (rows, cols)
    key = k_first + lax.broadcasted_iota(jnp.int32, shape, 1 - axis)
    ok = key >= low
    if causal:
        ok = ok & (key <= pos)
    return jnp.where(ok, 0.0, MASKED)


def bucket_cols(row):
    count = row.shape[1]
    return jnp.transpose(jnp.broadcast_to(row.astype(F32), (DIM, count))).astype(jnp.int32)


def lanes(rows):
    return lax.broadcasted_iota(jnp.int32, (rows, DIM), 1)


def one_hot(row):
    cols = bucket_cols(row)
    return jnp.where(cols == lanes(cols.shape[0]), 1.0, 0.0).astype(BF16)


def bias_rows(table_row, cols):
    gap = jnp.abs(cols - lanes(cols.shape[0]))
    spread = jnp.broadcast_to(table_row, gap.shape)
    return jnp.take_along_axis(spread, gap, axis=1).astype(BF16)


def bias_sum(mid, cols):
    lane = lanes(cols.shape[0])
    up, down = cols + lane, cols - lane
    above = jnp.take_along_axis(mid, up & (DIM - 1), axis=1)
    below = jnp.take_along_axis(mid, down & (DIM - 1), axis=1)
    both = jnp.where(up < DIM, above, 0.0) + jnp.where((down >= 0) & (lane > 0), below, 0.0)
    return jnp.sum(both, axis=0, keepdims=True) * 0.5


def attn_of(q_aug, k_aug, mask):
    half_score = dot_nt(q_aug, k_aug) * (0.5 * SCALE) + mask
    t = jnp.tanh(half_score)
    u = 1.0 + t
    return half_score * u, t, u


def back_of(q_aug, k_aug, mask, grad, value):
    attn, t, u = attn_of(q_aug, k_aug, mask)
    slope2 = u + attn * (1.0 - t)
    score_grad2 = (dot_nt(grad, value) * slope2).astype(BF16)
    return attn.astype(BF16), score_grad2


def cat(*parts):
    return jnp.concatenate(parts, axis=1)


def each_head(tab, base=0):
    for j in range(STEP):
        h = base + pl.program_id(0) * STEP + j
        yield h, slice(j * DIM, (j + 1) * DIM), tab[pl.ds(h, 1), :]


def own_forward_body(base, meta, q, k, v, bkt, tab, *rest):
    out, mask, hot, cols = rest[-4:]

    @pl.when(pl.program_id(0) == 0)
    def _():
        mask[...] = mask_tile(meta, meta[6], TOK, meta[6], TOK, True)
        hot[...] = one_hot(bkt[...])
        cols[...] = bucket_cols(bkt[...])

    for _, at, row in each_head(tab, base):
        q_aug = cat(q[:, at], bias_rows(row, cols[...]))
        k_aug = cat(k[:, at], hot[...])
        for i in range(2):
            lo, hi = i * HALF, (i + 1) * HALF
            attn, _, _ = attn_of(q_aug[lo:hi], k_aug[:hi], mask[lo:hi, :hi])
            out[lo:hi, at] = dot_nn(attn.astype(BF16), v[:hi, at])


def norm_of(mixed):
    mixed = mixed.astype(F32)
    center = jnp.mean(mixed, axis=1, keepdims=True)
    deviation = mixed - center
    variance = jnp.mean(deviation * deviation, axis=1, keepdims=True)
    inv_std = lax.rsqrt(variance + 1e-05)
    return deviation * inv_std, inv_std


def rows_body(
    meta, q, k, v, k_bkt, bkt, tab, partial, lifted, gate,
    gate_grad, gated, mixed_grad, total, mask, hot, cols,
):
    @pl.when(pl.program_id(0) == 0)
    def _():
        mask[...] = mask_tile(meta, meta[6], TOK, meta[6] - TOK, TOK, False)
        hot[...] = one_hot(k_bkt[0:1, :])
        cols[...] = bucket_cols(bkt[...])

    for h, at, row in each_head(tab):
        q_aug = cat(q[:, at], bias_rows(row, cols[...]))
        k_aug = cat(k[:, at], hot[...])
        column = pl.ds(pl.multiple_of(h * DIM, DIM), DIM)
        for i in range(2):
            lo, hi = i * HALF, (i + 1) * HALF
            attn, _, _ = attn_of(q_aug[lo:hi], k_aug[lo:], mask[lo:hi, lo:])
            total[lo:hi, column] = (
                partial[lo:hi, at] + dot_nn(attn.astype(BF16), v[lo:, at])
            ).astype(BF16)

    @pl.when(pl.program_id(0) == HEADS // STEP - 1)
    def _():
        @pl.loop(0, TOK // 64)
        def _(c):
            for i in range(2):
                rows = pl.ds(pl.multiple_of(c * 64 + i * 32, 32), 32)
                lift = lifted[rows, :]
                gate_f = gate[rows, :].astype(F32)
                normed, inv_std = norm_of(total[rows, :])
                gate_grad[rows, :] = (lift * normed).astype(BF16)
                gated[rows, :] = (normed * gate_f).astype(BF16)
                normed_grad = lift * gate_f
                mean_one = jnp.mean(normed_grad, axis=1, keepdims=True)
                mean_two = jnp.mean(normed_grad * normed, axis=1, keepdims=True)
                mixed_grad[rows, :] = (
                    inv_std * (normed_grad - mean_one - normed * mean_two)
                ).astype(BF16)


def lifted_body(meta, cot, users, owner, weight, lifted, total):
    @pl.when(pl.program_id(0) == 0)
    def _():
        count = users.shape[0]
        slot = lax.broadcasted_iota(jnp.int32, (DIM, count), 0)
        source = lax.broadcasted_iota(jnp.int32, (DIM, count), 1)
        pick = (owner[...] == meta[7] * 3 + (slot >> 3)) & ((source & 7) == (slot & 7)) & (slot < 24)
        rows = dot_nn(jnp.where(pick, 1.0, 0.0).astype(BF16), users[...]).astype(BF16)
        pos = meta[6] + lax.broadcasted_iota(jnp.int32, (TOK, 1), 0)
        lane = lanes(TOK)
        user = lane >> 3
        last = jnp.where(user == 0, meta[0], jnp.where(user == 1, meta[1], meta[2])) - 1
        hit = (pos == last) & (lane < 24)
        for c in range(WIDTH // DIM):
            at = slice(c * DIM, (c + 1) * DIM)
            hits = jnp.where(hit & ((lane & 7) == c), 1.0, 0.0).astype(BF16)
            total[:, at] = (cot[:, at].astype(F32) + dot_nn(hits, rows)).astype(BF16)

    lifted[...] = dot_nt(total[...], weight[...])


def weight_body(meta, gated, total, keep, send):
    part = dot_tn(gated[...], total[...])
    part = part.reshape(4, 2, 32, WIDTH)

    @pl.when(meta[8] == 0)
    def _():
        keep[...] = part[:, 0]
        send[...] = part[:, 1].astype(BF16)

    @pl.when(meta[8] == 1)
    def _():
        keep[...] = part[:, 1]
        send[...] = part[:, 0].astype(BF16)


def own_backward_body(
    meta, q, k, v, kh, vh, kh_bkt, bkt, tab, grad,
    dq, dk, dv, bias, mask, mask_h, hot, hot_h, cols,
):
    @pl.when(pl.program_id(0) == 0)
    def _():
        mask[...] = mask_tile(meta, meta[6], TOK, meta[6], TOK, True, True)
        mask_h[...] = mask_tile(meta, meta[6], TOK, meta[6] - TOK, TOK, False)
        hot[...] = one_hot(bkt[...])
        hot_h[...] = one_hot(kh_bkt[0:1, :])
        cols[...] = bucket_cols(bkt[...])

    for h, at, row in each_head(tab):
        own_backward_head(
            q[:, at], k[:, at], v[:, at], kh[:, at], vh[:, at], row, grad[:, at],
            dq, dk, dv, bias, mask, mask_h, hot, hot_h, cols, h, at,
        )


def own_backward_head(
    q, k, v, kh, vh, row, grad, dq, dk, dv, bias, mask, mask_h, hot, hot_h, cols, h, at
):
    q_aug = cat(q, bias_rows(row, cols[...]))
    k_aug = cat(k, hot[...])
    kh_aug = cat(kh, hot_h[...])
    ge, gl = grad[:HALF], grad[HALF:]
    attn, sg = back_of(k_aug[:HALF], q_aug, mask[:HALF, :], v[:HALF], grad)
    dk[:HALF, at] = dot_nn(sg, q)
    dv[:HALF, at] = dot_nn(attn, grad)
    own = dot_tn(sg, k_aug[:HALF])
    early, late = own[:HALF], own[HALF:]
    attn, sg = back_of(k_aug[HALF:], q_aug[HALF:], mask[HALF:, HALF:], v[HALF:], gl)
    dk[HALF:, at] = dot_nn(sg, q[HALF:])
    dv[HALF:, at] = dot_nn(attn, gl)
    late = late + dot_tn(sg, k_aug[HALF:])
    _, sg = back_of(q_aug[:HALF], kh_aug, mask_h[:HALF, :], ge, vh)
    early = early + dot_nn(sg, kh_aug)
    _, sg = back_of(q_aug[HALF:], kh_aug[HALF:], mask_h[HALF:, HALF:], gl, vh[HALF:])
    late = late + dot_nn(sg, kh_aug[HALF:])
    dq[:HALF, at] = (early[:, :DIM] * (0.5 * SCALE)).astype(BF16)
    dq[HALF:, at] = (late[:, :DIM] * (0.5 * SCALE)).astype(BF16)
    bias[pl.ds(h, 1), :] = bias_sum(early[:, DIM:], cols[:HALF, :]) + bias_sum(late[:, DIM:], cols[HALF:, :])


def sent_backward_body(
    base, meta, qs, q_bkt, grad, k, v, bkt, tab, dk_own, dv_own, *rest
):
    dk, dv, mask, mask_l, hot, cols = rest[-6:]

    @pl.when(pl.program_id(0) == 0)
    def _():
        mask[...] = mask_tile(meta, meta[6] + TOK, HALF, meta[6], TOK, False, True)
        mask_l[...] = mask_tile(meta, meta[6] + TOK + HALF, HALF, meta[6] + HALF, HALF, False, True)
        hot[...] = one_hot(bkt[...])
        cols[...] = bucket_cols(q_bkt[...])

    for _, at, row in each_head(tab, base):
        added = bias_rows(row, cols[...])
        k_aug = cat(k[:, at], hot[...])
        ge, gl = grad[:HALF, at], grad[HALF:, at]
        qe, ql = qs[:HALF, at], qs[HALF:, at]
        attn, sg = back_of(k_aug, cat(qe, added[:HALF]), mask[...], v[:, at], ge)
        sum_k = dk_own[:, at] + dot_nn(sg, qe)
        sum_v = dv_own[:, at] + dot_nn(attn, ge)
        attn, sg = back_of(k_aug[HALF:], cat(ql, added[HALF:]), mask_l[...], v[HALF:, at], gl)
        dk[:HALF, at] = (sum_k[:HALF] * (0.5 * SCALE)).astype(BF16)
        dv[:HALF, at] = sum_v[:HALF].astype(BF16)
        dk[HALF:, at] = ((sum_k[HALF:] + dot_nn(sg, ql)) * (0.5 * SCALE)).astype(BF16)
        dv[HALF:, at] = (sum_v[HALF:] + dot_nn(attn, gl)).astype(BF16)


SMEM = pl.BlockSpec(memory_space=pltpu.SMEM)


def heads_of(rows, at=0):
    return pl.BlockSpec((rows, STEP * DIM), lambda h: (at, h))


def whole(*shape):
    return pl.BlockSpec(shape, lambda h: (0,) * len(shape))


def shape_of(rows, kind, cols=WIDTH):
    return jax.ShapeDtypeStruct((rows, cols), kind)


def call(body, name, grid, in_specs, out_specs, out_shape, scratch=(), aliases=None, flops=0, moved=0):
    return pl.pallas_call(
        body,
        name=name,
        grid=grid,
        in_specs=in_specs,
        out_specs=out_specs,
        out_shape=out_shape,
        scratch_shapes=list(scratch),
        input_output_aliases=aliases or {},
        cost_estimate=pl.CostEstimate(flops=flops // COST, bytes_accessed=moved // COST, transcendentals=0),
        compiler_params=pltpu.CompilerParams(vmem_limit_bytes=VMEM_LIMIT),
    )


def on_device(
    query_rows, key_rows, value_rows, gate_rows, out_grad, out_weight,
    time_bias, time_bucket, lengths, band_width, user_grad, user_owner,
):
    q, k, v = query_rows[0], key_rows[0], value_rows[0]
    gate, cot = gate_rows[0], out_grad[0]
    bkt = time_bucket
    ctx = lax.axis_index("ctx")
    rank = lax.axis_index("rank")
    n_ctx = lax.axis_size("ctx")
    n_dp = lax.axis_size("dp")
    section = lax.axis_index("dp") * lax.axis_size("rank") + rank
    ends = jnp.cumsum(lengths[0])
    first = ctx * TOK
    meta = jnp.concatenate(
        [ends, band_width[0], jnp.stack([first, section, rank])]
    ).astype(jnp.int32)
    tab = time_bias.astype(F32) * math.sqrt(DIM)
    up = [(i, i + 1) for i in range(n_ctx - 1)]
    down = [(i + 1, i) for i in range(n_ctx - 1)]

    bkt_rows = jnp.pad(jnp.broadcast_to(bkt.astype(BF16), (PAD, TOK)), ((0, 0), (0, WIDTH - TOK)))
    kv_came = lax.ppermute(jnp.concatenate([k, v, bkt_rows]), "ctx", up)
    q_came = lax.ppermute(q, "ctx", down)
    bkt_after = lax.ppermute(bkt, "ctx", down)
    owner = jnp.pad(
        jnp.repeat(user_owner.reshape(-1, 3), 8, axis=1), ((0, 0), (0, 8)), constant_values=-1
    ).reshape(1, WIDTH)

    came_bkt = pl.BlockSpec((PAD, TOK), lambda h: (2 * TOK // PAD, 0))
    col = pltpu.VMEM((TOK, DIM), jnp.int32)
    hot = pltpu.VMEM((TOK, DIM), BF16)

    own_half = functools.partial(
        call, grid=(HEADS // STEP // 2,), out_shape=shape_of(TOK, F32),
        scratch=[pltpu.VMEM((TOK, TOK), F32), hot, col], flops=2_000_000_000, moved=3 << 20,
    )
    shift = HEADS // STEP // 2
    lower = pl.BlockSpec((TOK, STEP * DIM), lambda h: (0, h))
    upper = pl.BlockSpec((TOK, STEP * DIM), lambda h: (0, h + shift))
    own_out = own_half(
        functools.partial(own_forward_body, 0), "own_forward_low",
        in_specs=[SMEM, lower, lower, lower, whole(1, TOK), whole(HEADS, DIM)], out_specs=lower,
    )(meta, q, k, v, bkt, tab)

    pieces = jnp.pad(user_grad.reshape(24, DIM), ((0, 8), (0, 0)))
    half_weight = lax.dynamic_slice_in_dim(out_weight, rank * 32, 32)
    shared = jnp.concatenate([half_weight, pieces], axis=1)
    weight = lax.all_to_all(
        jnp.broadcast_to(shared[None], (2 * n_dp, 32, WIDTH + DIM)), ("dp", "rank"), 0, 0, tiled=True
    ).reshape(WIDTH, WIDTH + DIM)

    own_out = own_half(
        functools.partial(own_forward_body, HEADS // 2), "own_forward_high",
        in_specs=[SMEM, upper, upper, upper, whole(1, TOK), whole(HEADS, DIM),
                  pl.BlockSpec(memory_space=pl.ANY)],
        out_specs=upper, aliases={6: 0},
    )(meta, q, k, v, bkt, tab, own_out)

    lifted, total = call(
        lifted_body, "lifted", (4,),
        [SMEM, whole(TOK, WIDTH), pl.BlockSpec((WIDTH, DIM), lambda h: (0, WIDTH // DIM)),
         whole(1, WIDTH), pl.BlockSpec((HALF, WIDTH), lambda h: (h, 0))],
        (pl.BlockSpec((TOK, HALF), lambda h: (0, h)), whole(TOK, WIDTH)),
        (shape_of(TOK, F32), shape_of(TOK, BF16)),
        flops=1_200_000_000, moved=6 << 20,
    )(meta, cot, weight, owner, weight)

    meta_rows, q_came, bkt_after = lax.optimization_barrier((meta, q_came, bkt_after))
    gate_grad, gated, grad = call(
        rows_body, "rows", (HEADS // STEP,),
        [SMEM, heads_of(TOK), heads_of(TOK), heads_of(TOK, 1), came_bkt, whole(1, TOK),
         whole(HEADS, DIM), heads_of(TOK), whole(TOK, WIDTH), whole(TOK, WIDTH)],
        (whole(TOK, WIDTH),) * 3,
        (shape_of(TOK, BF16),) * 3,
        [pltpu.VMEM((TOK, WIDTH), BF16), pltpu.VMEM((TOK, TOK), F32), hot, col],
        flops=2_000_000_000, moved=10 << 20,
    )(meta_rows, q, kv_came, kv_came, kv_came, bkt, tab, own_out, lifted, gate)
    grad_came = lax.ppermute(grad, "ctx", down)

    cut = pl.BlockSpec((TOK, HALF), lambda h: (0, h))
    piece = pl.BlockSpec((4, 32, WIDTH), lambda h: (h, 0, 0))
    keep, send = call(
        weight_body, "weight_part", (4,),
        [SMEM, cut, whole(TOK, WIDTH)],
        (piece, piece),
        (jax.ShapeDtypeStruct((16, 32, WIDTH), F32), jax.ShapeDtypeStruct((16, 32, WIDTH), BF16)),
        flops=1_100_000_000, moved=6 << 20,
    )(meta, gated, total)
    other = lax.ppermute(send, "rank", [(0, 1), (1, 0)])
    other, meta_own = lax.optimization_barrier((other, meta))
    passed = pl.BlockSpec(memory_space=pl.ANY)

    dq, dk_own, dv_own, bias = call(
        own_backward_body, "own_backward", (HEADS // STEP,),
        [SMEM] + [heads_of(TOK)] * 4 + [heads_of(TOK, 1), came_bkt, whole(1, TOK), whole(HEADS, DIM), heads_of(TOK)],
        (heads_of(TOK), heads_of(TOK), heads_of(TOK), whole(HEADS, DIM)),
        (shape_of(TOK, BF16), shape_of(TOK, F32), shape_of(TOK, F32), shape_of(HEADS, F32, DIM)),
        [pltpu.VMEM((TOK, TOK), F32), pltpu.VMEM((TOK, TOK), F32), hot, hot, col],
        flops=10_000_000_000, moved=12 << 20,
    )(meta_own, q, k, v, kv_came, kv_came, kv_came, bkt, tab, grad)

    flat = bias.reshape(1, WIDTH)
    high = flat.astype(BF16)
    low = (flat - high.astype(F32)).astype(BF16)
    extra = jnp.concatenate([high, low, jnp.zeros((6, WIDTH), BF16)], axis=0)
    pair = jnp.concatenate(
        [(keep + other.astype(F32)).astype(BF16), jnp.broadcast_to(extra[None], (n_dp, 8, WIDTH))], axis=1
    )
    rows = lax.all_to_all(pair, "dp", 0, 0, tiled=True)

    def sent_all(meta):
        return call(
            functools.partial(sent_backward_body, 0), "sent_backward", (HEADS // STEP,),
            [SMEM, heads_of(TOK), whole(1, TOK)] + [heads_of(TOK)] * 3
            + [whole(1, TOK), whole(HEADS, DIM), heads_of(TOK), heads_of(TOK)],
            (heads_of(TOK), heads_of(TOK)),
            (shape_of(TOK, BF16), shape_of(TOK, BF16)),
            [pltpu.VMEM((TOK, HALF), F32), pltpu.VMEM((HALF, HALF), F32), hot, col],
            flops=4_000_000_000, moved=10 << 20,
        )(meta, q_came, bkt_after, grad_came, k, v, bkt, tab, dk_own, dv_own)

    dk, dv = sent_all(meta)
    rows, dk, dv = lax.optimization_barrier((rows, dk, dv))
    rows = jnp.sum(rows.astype(F32), axis=0)
    high = rows.astype(BF16)
    row = rows[32:33] + rows[33:34]
    top = row.astype(BF16)
    rest = (row - top.astype(F32)).astype(BF16)
    rows = jnp.concatenate([high[:32], top, rest, high[34:]], axis=0)
    rows = lax.all_to_all(
        jnp.broadcast_to(rows[None], (2 * n_ctx,) + rows.shape), ("ctx", "rank"), 0, 0, tiled=True
    )
    rows = jnp.sum(rows.reshape(n_ctx, 2, 40, WIDTH).astype(F32), axis=0)
    weight_grad = rows[:, :32].reshape(64, WIDTH)
    last = rows[0, 32] + rows[1, 32] + rows[0, 33] + rows[1, 33]
    bias_grad = lax.dynamic_slice_in_dim(last.reshape(HEADS, DIM), ctx, 1)
    return (dq[None], dk[None], dv[None], gate_grad[None], weight_grad, bias_grad)


def solution(mesh):
    rows = P(("dp", "rank"), "ctx", None)
    users = P(("dp", "rank"), None)
    return jax.shard_map(
        on_device,
        mesh=mesh,
        in_specs=(
            rows, rows, rows, rows, rows, P("dp", None), P(), P(("dp", "rank"), "ctx"),
            users, users, users, P(),
        ),
        out_specs=(rows, rows, rows, rows, P("dp", None), P("ctx", None)),
        check_vma=False,
    )
```

```python
import functools
import math

import jax
import jax.numpy as jnp
from jax import lax
from jax.experimental import pallas as pl
from jax.experimental.pallas import tpu as pltpu
from jax.sharding import PartitionSpec as P

F32 = jnp.float32
BF16 = jnp.bfloat16
HEADS = 8
DIM = 128
TOK = 512
HALF = 256
WIDTH = 1024
MASKED = -1e9
SCALE = 1.0 / math.sqrt(DIM)
STEP = 2
COST = 1
VMEM_LIMIT = 60 * 1024 * 1024


def dot_nt(a, b):
    return lax.dot_general(a, b, (((1,), (1,)), ((), ())), preferred_element_type=F32)


def dot_nn(a, b):
    return lax.dot_general(a, b, (((1,), (0,)), ((), ())), preferred_element_type=F32)


def dot_tn(a, b):
    return lax.dot_general(a, b, (((0,), (0,)), ((), ())), preferred_element_type=F32)


def lowest_key(meta, first, rows, axis=0):
    shape = (rows, 1) if axis == 0 else (1, rows)
    pos = first + lax.broadcasted_iota(jnp.int32, shape, axis)
    e0, e1, e2 = meta[0], meta[1], meta[2]
    start = jnp.where(pos >= e0, e0, 0)
    band = jnp.where(pos >= e0, meta[4], meta[3])
    start = jnp.where(pos >= e1, e1, start)
    band = jnp.where(pos >= e1, meta[5], band)
    start = jnp.where(pos >= e2, e2, start)
    band = jnp.where(pos >= e2, 0, band)
    return pos, jnp.maximum(start, pos - band + 1)


def mask_tile(meta, q_first, rows, k_first, cols, causal, turned=False):
    axis = 1 if turned else 0
    pos, low = lowest_key(meta, q_first, rows, axis)
    shape = (cols, rows) if turned else (rows, cols)
    key = k_first + lax.broadcasted_iota(jnp.int32, shape, 1 - axis)
    ok = key >= low
    if causal:
        ok = ok & (key <= pos)
    return jnp.where(ok, 0.0, MASKED)


def bucket_cols(row):
    count = row.shape[1]
    return jnp.transpose(jnp.broadcast_to(row.astype(F32), (DIM, count))).astype(jnp.int32)


def lanes(rows):
    return lax.broadcasted_iota(jnp.int32, (rows, DIM), 1)


def one_hot(row):
    cols = bucket_cols(row)
    return jnp.where(cols == lanes(cols.shape[0]), 1.0, 0.0).astype(BF16)


def bias_rows(table_row, cols):
    gap = jnp.abs(cols - lanes(cols.shape[0]))
    spread = jnp.broadcast_to(table_row, gap.shape)
    return jnp.take_along_axis(spread, gap, axis=1).astype(BF16)


def bias_sum(mid, cols):
    lane = lanes(cols.shape[0])
    up, down = cols + lane, cols - lane
    above = jnp.take_along_axis(mid, up & (DIM - 1), axis=1)
    below = jnp.take_along_axis(mid, down & (DIM - 1), axis=1)
    both = jnp.where(up < DIM, above, 0.0) + jnp.where((down >= 0) & (lane > 0), below, 0.0)
    return jnp.sum(both, axis=0, keepdims=True) * 0.5


def attn_of(q_aug, k_aug, mask):
    half_score = dot_nt(q_aug, k_aug) * (0.5 * SCALE) + mask
    t = jnp.tanh(half_score)
    u = 1.0 + t
    return half_score * u, t, u


def back_of(q_aug, k_aug, mask, grad, value):
    attn, t, u = attn_of(q_aug, k_aug, mask)
    slope2 = u + attn * (1.0 - t)
    score_grad2 = (dot_nt(grad, value) * slope2).astype(BF16)
    return attn.astype(BF16), score_grad2


def cat(*parts):
    return jnp.concatenate(parts, axis=1)


def each_head(tab, base=0):
    for j in range(STEP):
        h = base + pl.program_id(0) * STEP + j
        yield h, slice(j * DIM, (j + 1) * DIM), tab[pl.ds(h, 1), :]


def own_forward_body(base, meta, q, k, v, bkt, tab, *rest):
    out, mask, hot, cols = rest[-4:]

    @pl.when(pl.program_id(0) == 0)
    def _():
        mask[...] = mask_tile(meta, meta[6], TOK, meta[6], TOK, True)
        hot[...] = one_hot(bkt[...])
        cols[...] = bucket_cols(bkt[...])

    for _, at, row in each_head(tab, base):
        q_aug = cat(q[:, at], bias_rows(row, cols[...]))
        k_aug = cat(k[:, at], hot[...])
        for i in range(2):
            lo, hi = i * HALF, (i + 1) * HALF
            attn, _, _ = attn_of(q_aug[lo:hi], k_aug[:hi], mask[lo:hi, :hi])
            out[lo:hi, at] = dot_nn(attn.astype(BF16), v[:hi, at])


def norm_of(mixed):
    mixed = mixed.astype(F32)
    center = jnp.mean(mixed, axis=1, keepdims=True)
    deviation = mixed - center
    variance = jnp.mean(deviation * deviation, axis=1, keepdims=True)
    inv_std = lax.rsqrt(variance + 1e-05)
    return deviation * inv_std, inv_std


def rows_body(
    meta, q, k, v, k_bkt, bkt, tab, partial, lifted, gate,
    gate_grad, gated, mixed_grad, total, mask, hot, cols,
):
    @pl.when(pl.program_id(0) == 0)
    def _():
        mask[...] = mask_tile(meta, meta[6], TOK, meta[6] - TOK, TOK, False)
        hot[...] = one_hot(k_bkt[...])
        cols[...] = bucket_cols(bkt[...])

    for h, at, row in each_head(tab):
        q_aug = cat(q[:, at], bias_rows(row, cols[...]))
        k_aug = cat(k[:, at], hot[...])
        column = pl.ds(pl.multiple_of(h * DIM, DIM), DIM)
        for i in range(2):
            lo, hi = i * HALF, (i + 1) * HALF
            attn, _, _ = attn_of(q_aug[lo:hi], k_aug[lo:], mask[lo:hi, lo:])
            total[lo:hi, column] = (
                partial[lo:hi, at] + dot_nn(attn.astype(BF16), v[lo:, at])
            ).astype(BF16)

    @pl.when(pl.program_id(0) == HEADS // STEP - 1)
    def _():
        @pl.loop(0, TOK // 64)
        def _(c):
            for i in range(2):
                rows = pl.ds(pl.multiple_of(c * 64 + i * 32, 32), 32)
                lift = lifted[rows, :]
                gate_f = gate[rows, :].astype(F32)
                normed, inv_std = norm_of(total[rows, :])
                gate_grad[rows, :] = (lift * normed).astype(BF16)
                gated[rows, :] = (normed * gate_f).astype(BF16)
                normed_grad = lift * gate_f
                mean_one = jnp.mean(normed_grad, axis=1, keepdims=True)
                mean_two = jnp.mean(normed_grad * normed, axis=1, keepdims=True)
                mixed_grad[rows, :] = (
                    inv_std * (normed_grad - mean_one - normed * mean_two)
                ).astype(BF16)


def lifted_body(meta, cot, users, owner, weight, lifted, total):
    @pl.when(pl.program_id(0) == 0)
    def _():
        count = users.shape[0]
        slot = lax.broadcasted_iota(jnp.int32, (DIM, count), 0)
        source = lax.broadcasted_iota(jnp.int32, (DIM, count), 1)
        pick = (owner[...] == meta[7] * 3 + (slot >> 3)) & ((source & 7) == (slot & 7)) & (slot < 24)
        rows = dot_nn(jnp.where(pick, 1.0, 0.0).astype(BF16), users[...]).astype(BF16)
        pos = meta[6] + lax.broadcasted_iota(jnp.int32, (TOK, 1), 0)
        lane = lanes(TOK)
        user = lane >> 3
        last = jnp.where(user == 0, meta[0], jnp.where(user == 1, meta[1], meta[2])) - 1
        hit = (pos == last) & (lane < 24)
        for c in range(WIDTH // DIM):
            at = slice(c * DIM, (c + 1) * DIM)
            hits = jnp.where(hit & ((lane & 7) == c), 1.0, 0.0).astype(BF16)
            total[:, at] = (cot[:, at].astype(F32) + dot_nn(hits, rows)).astype(BF16)

    lifted[...] = dot_nt(total[...], weight[...])


def weight_body(meta, gated, total, keep, send):
    part = dot_tn(gated[...], total[...])
    part = part.reshape(4, 2, 32, WIDTH)

    @pl.when(meta[8] == 0)
    def _():
        keep[...] = part[:, 0]
        send[...] = part[:, 1].astype(BF16)

    @pl.when(meta[8] == 1)
    def _():
        keep[...] = part[:, 1]
        send[...] = part[:, 0].astype(BF16)


def own_backward_body(
    meta, q, k, v, kh, vh, kh_bkt, bkt, tab, grad,
    dq, dk, dv, bias, mask, mask_h, hot, hot_h, cols,
):
    @pl.when(pl.program_id(0) == 0)
    def _():
        mask[...] = mask_tile(meta, meta[6], TOK, meta[6], TOK, True, True)
        mask_h[...] = mask_tile(meta, meta[6], TOK, meta[6] - TOK, TOK, False)
        hot[...] = one_hot(bkt[...])
        hot_h[...] = one_hot(kh_bkt[...])
        cols[...] = bucket_cols(bkt[...])

    for h, at, row in each_head(tab):
        own_backward_head(
            q[:, at], k[:, at], v[:, at], kh[:, at], vh[:, at], row, grad[:, at],
            dq, dk, dv, bias, mask, mask_h, hot, hot_h, cols, h, at,
        )


def own_backward_head(
    q, k, v, kh, vh, row, grad, dq, dk, dv, bias, mask, mask_h, hot, hot_h, cols, h, at
):
    q_aug = cat(q, bias_rows(row, cols[...]))
    k_aug = cat(k, hot[...])
    kh_aug = cat(kh, hot_h[...])
    ge, gl = grad[:HALF], grad[HALF:]
    attn, sg = back_of(k_aug[:HALF], q_aug, mask[:HALF, :], v[:HALF], grad)
    dk[:HALF, at] = dot_nn(sg, q)
    dv[:HALF, at] = dot_nn(attn, grad)
    own = dot_tn(sg, k_aug[:HALF])
    early, late = own[:HALF], own[HALF:]
    attn, sg = back_of(k_aug[HALF:], q_aug[HALF:], mask[HALF:, HALF:], v[HALF:], gl)
    dk[HALF:, at] = dot_nn(sg, q[HALF:])
    dv[HALF:, at] = dot_nn(attn, gl)
    late = late + dot_tn(sg, k_aug[HALF:])
    _, sg = back_of(q_aug[:HALF], kh_aug, mask_h[:HALF, :], ge, vh)
    early = early + dot_nn(sg, kh_aug)
    _, sg = back_of(q_aug[HALF:], kh_aug[HALF:], mask_h[HALF:, HALF:], gl, vh[HALF:])
    late = late + dot_nn(sg, kh_aug[HALF:])
    dq[:HALF, at] = (early[:, :DIM] * (0.5 * SCALE)).astype(BF16)
    dq[HALF:, at] = (late[:, :DIM] * (0.5 * SCALE)).astype(BF16)
    bias[pl.ds(h, 1), :] = bias_sum(early[:, DIM:], cols[:HALF, :]) + bias_sum(late[:, DIM:], cols[HALF:, :])


def sent_backward_body(
    base, meta, qs, q_bkt, grad, k, v, bkt, tab, dk_own, dv_own, *rest
):
    dk, dv, mask, mask_l, hot, cols = rest[-6:]

    @pl.when(pl.program_id(0) == 0)
    def _():
        mask[...] = mask_tile(meta, meta[6] + TOK, HALF, meta[6], TOK, False, True)
        mask_l[...] = mask_tile(meta, meta[6] + TOK + HALF, HALF, meta[6] + HALF, HALF, False, True)
        hot[...] = one_hot(bkt[...])
        cols[...] = bucket_cols(q_bkt[...])

    for _, at, row in each_head(tab, base):
        added = bias_rows(row, cols[...])
        k_aug = cat(k[:, at], hot[...])
        ge, gl = grad[:HALF, at], grad[HALF:, at]
        qe, ql = qs[:HALF, at], qs[HALF:, at]
        attn, sg = back_of(k_aug, cat(qe, added[:HALF]), mask[...], v[:, at], ge)
        sum_k = dk_own[:, at] + dot_nn(sg, qe)
        sum_v = dv_own[:, at] + dot_nn(attn, ge)
        attn, sg = back_of(k_aug[HALF:], cat(ql, added[HALF:]), mask_l[...], v[HALF:, at], gl)
        dk[:HALF, at] = (sum_k[:HALF] * (0.5 * SCALE)).astype(BF16)
        dv[:HALF, at] = sum_v[:HALF].astype(BF16)
        dk[HALF:, at] = ((sum_k[HALF:] + dot_nn(sg, ql)) * (0.5 * SCALE)).astype(BF16)
        dv[HALF:, at] = (sum_v[HALF:] + dot_nn(attn, gl)).astype(BF16)


SMEM = pl.BlockSpec(memory_space=pltpu.SMEM)


def heads_of(rows, at=0):
    return pl.BlockSpec((rows, STEP * DIM), lambda h: (at, h))


def whole(*shape):
    return pl.BlockSpec(shape, lambda h: (0,) * len(shape))


def shape_of(rows, kind, cols=WIDTH):
    return jax.ShapeDtypeStruct((rows, cols), kind)


def call(body, name, grid, in_specs, out_specs, out_shape, scratch=(), aliases=None, flops=0, moved=0):
    return pl.pallas_call(
        body,
        name=name,
        grid=grid,
        in_specs=in_specs,
        out_specs=out_specs,
        out_shape=out_shape,
        scratch_shapes=list(scratch),
        input_output_aliases=aliases or {},
        cost_estimate=pl.CostEstimate(flops=flops // COST, bytes_accessed=moved // COST, transcendentals=0),
        compiler_params=pltpu.CompilerParams(vmem_limit_bytes=VMEM_LIMIT),
    )


def on_device(
    query_rows, key_rows, value_rows, gate_rows, out_grad, out_weight,
    time_bias, time_bucket, lengths, band_width, user_grad, user_owner,
):
    q, k, v = query_rows[0], key_rows[0], value_rows[0]
    gate, cot = gate_rows[0], out_grad[0]
    bkt = time_bucket
    ctx = lax.axis_index("ctx")
    rank = lax.axis_index("rank")
    n_ctx = lax.axis_size("ctx")
    n_dp = lax.axis_size("dp")
    section = lax.axis_index("dp") * lax.axis_size("rank") + rank
    ends = jnp.cumsum(lengths[0])
    first = ctx * TOK
    meta = jnp.concatenate(
        [ends, band_width[0], jnp.stack([first, section, rank])]
    ).astype(jnp.int32)
    tab = time_bias.astype(F32) * math.sqrt(DIM)
    up = [(i, i + 1) for i in range(n_ctx - 1)]
    down = [(i + 1, i) for i in range(n_ctx - 1)]

    k_came = lax.ppermute(k, "ctx", up)
    v_came = lax.ppermute(v, "ctx", up)
    q_came = lax.ppermute(q, "ctx", down)
    bkt_before = lax.ppermute(bkt, "ctx", up)
    bkt_after = lax.ppermute(bkt, "ctx", down)
    owner = jnp.pad(
        jnp.repeat(user_owner.reshape(-1, 3), 8, axis=1), ((0, 0), (0, 8)), constant_values=-1
    ).reshape(1, WIDTH)

    col = pltpu.VMEM((TOK, DIM), jnp.int32)
    hot = pltpu.VMEM((TOK, DIM), BF16)

    own_half = functools.partial(
        call, grid=(HEADS // STEP // 2,), out_shape=shape_of(TOK, F32),
        scratch=[pltpu.VMEM((TOK, TOK), F32), hot, col], flops=2_000_000_000, moved=3 << 20,
    )
    shift = HEADS // STEP // 2
    lower = pl.BlockSpec((TOK, STEP * DIM), lambda h: (0, h))
    upper = pl.BlockSpec((TOK, STEP * DIM), lambda h: (0, h + shift))
    own_out = own_half(
        functools.partial(own_forward_body, 0), "own_forward_low",
        in_specs=[SMEM, lower, lower, lower, whole(1, TOK), whole(HEADS, DIM)], out_specs=lower,
    )(meta, q, k, v, bkt, tab)

    pieces = jnp.pad(user_grad.reshape(24, DIM), ((0, 8), (0, 0)))
    half_weight = lax.dynamic_slice_in_dim(out_weight, rank * 32, 32)
    shared = jnp.concatenate([half_weight, pieces], axis=1)
    weight = lax.all_to_all(
        jnp.broadcast_to(shared[None], (2 * n_dp, 32, WIDTH + DIM)), ("dp", "rank"), 0, 0, tiled=True
    ).reshape(WIDTH, WIDTH + DIM)

    own_out = own_half(
        functools.partial(own_forward_body, HEADS // 2), "own_forward_high",
        in_specs=[SMEM, upper, upper, upper, whole(1, TOK), whole(HEADS, DIM),
                  pl.BlockSpec(memory_space=pl.ANY)],
        out_specs=upper, aliases={6: 0},
    )(meta, q, k, v, bkt, tab, own_out)

    lifted, total = call(
        lifted_body, "lifted", (4,),
        [SMEM, whole(TOK, WIDTH), pl.BlockSpec((WIDTH, DIM), lambda h: (0, WIDTH // DIM)),
         whole(1, WIDTH), pl.BlockSpec((HALF, WIDTH), lambda h: (h, 0))],
        (pl.BlockSpec((TOK, HALF), lambda h: (0, h)), whole(TOK, WIDTH)),
        (shape_of(TOK, F32), shape_of(TOK, BF16)),
        flops=1_200_000_000, moved=6 << 20,
    )(meta, cot, weight, owner, weight)

    meta_rows, q_came, bkt_after = lax.optimization_barrier((meta, q_came, bkt_after))
    gate_grad, gated, grad = call(
        rows_body, "rows", (HEADS // STEP,),
        [SMEM, heads_of(TOK), heads_of(TOK), heads_of(TOK), whole(1, TOK), whole(1, TOK),
         whole(HEADS, DIM), heads_of(TOK), whole(TOK, WIDTH), whole(TOK, WIDTH)],
        (whole(TOK, WIDTH),) * 3,
        (shape_of(TOK, BF16),) * 3,
        [pltpu.VMEM((TOK, WIDTH), BF16), pltpu.VMEM((TOK, TOK), F32), hot, col],
        flops=2_000_000_000, moved=10 << 20,
    )(meta_rows, q, k_came, v_came, bkt_before, bkt, tab, own_out, lifted, gate)
    grad_came = lax.ppermute(grad, "ctx", down)

    cut = pl.BlockSpec((TOK, HALF), lambda h: (0, h))
    piece = pl.BlockSpec((4, 32, WIDTH), lambda h: (h, 0, 0))
    keep, send = call(
        weight_body, "weight_part", (4,),
        [SMEM, cut, whole(TOK, WIDTH)],
        (piece, piece),
        (jax.ShapeDtypeStruct((16, 32, WIDTH), F32), jax.ShapeDtypeStruct((16, 32, WIDTH), BF16)),
        flops=1_100_000_000, moved=6 << 20,
    )(meta, gated, total)
    other = lax.ppermute(send, "rank", [(0, 1), (1, 0)])
    pair = (keep + other.astype(F32)).astype(BF16)
    rows = lax.all_to_all(pair, "dp", 0, 0, tiled=True)
    meta_own, _ = lax.optimization_barrier((meta, pair))
    passed = pl.BlockSpec(memory_space=pl.ANY)

    dq, dk_own, dv_own, bias = call(
        own_backward_body, "own_backward", (HEADS // STEP,),
        [SMEM] + [heads_of(TOK)] * 5 + [whole(1, TOK), whole(1, TOK), whole(HEADS, DIM), heads_of(TOK)],
        (heads_of(TOK), heads_of(TOK), heads_of(TOK), whole(HEADS, DIM)),
        (shape_of(TOK, BF16), shape_of(TOK, F32), shape_of(TOK, F32), shape_of(HEADS, F32, DIM)),
        [pltpu.VMEM((TOK, TOK), F32), pltpu.VMEM((TOK, TOK), F32), hot, hot, col],
        flops=10_000_000_000, moved=12 << 20,
    )(meta_own, q, k, v, k_came, v_came, bkt_before, bkt, tab, grad)

    spread = jnp.broadcast_to(bias[None, :, None], (n_dp, n_ctx, 2, DIM)).reshape(-1, DIM)
    rows, spread, grad_came = lax.optimization_barrier((rows, spread, grad_came))
    bias_all = lax.all_to_all(spread, ("dp", "ctx", "rank"), 0, 0, tiled=True)
    rows = jnp.sum(rows.astype(F32), axis=0)
    def sent_half(at, meta, *done):
        cols = functools.partial(pl.BlockSpec, index_map=lambda h: (0, h + at))
        out = cols((TOK, STEP * DIM))
        return call(
            functools.partial(sent_backward_body, at * STEP), "sent_backward", (HEADS // STEP // 2,),
            [SMEM, out, whole(1, TOK), out, out, out, whole(1, TOK), whole(HEADS, DIM), out, out]
            + [passed] * len(done),
            (out, out),
            (shape_of(TOK, BF16), shape_of(TOK, BF16)),
            [pltpu.VMEM((TOK, HALF), F32), pltpu.VMEM((HALF, HALF), F32), hot, col],
            aliases={10: 0, 11: 1} if done else None,
            flops=2_000_000_000, moved=5 << 20,
        )(meta, q_came, bkt_after, grad_came, k, v, bkt, tab, dk_own, dv_own, *done)

    def add_swap(rows, bit):
        return rows + lax.ppermute(rows, "ctx", [(i, i ^ bit) for i in range(n_ctx)])

    rows, meta_back = lax.optimization_barrier((rows, meta))
    done = sent_half(0, meta_back)
    rows = add_swap(rows, 4)
    rows, meta_back, *done = lax.optimization_barrier((rows, meta, *done))
    dk, dv = sent_half(HEADS // STEP // 2, meta_back, *done)
    rows = add_swap(rows, 2)
    rows, dk, dv = lax.optimization_barrier((rows, dk, dv))
    rows = add_swap(rows, 1)
    rows, bias_all = lax.optimization_barrier((rows, bias_all))
    other_rows = lax.ppermute(rows, "rank", [(0, 1), (1, 0)])
    weight_grad = jnp.concatenate(
        [jnp.where(rank == 0, rows, other_rows), jnp.where(rank == 0, other_rows, rows)], axis=0
    )
    bias_grad = jnp.sum(bias_all, axis=0, keepdims=True)
    return (dq[None], dk[None], dv[None], gate_grad[None], weight_grad, bias_grad)


def solution(mesh):
    rows = P(("dp", "rank"), "ctx", None)
    users = P(("dp", "rank"), None)
    return jax.shard_map(
        on_device,
        mesh=mesh,
        in_specs=(
            rows, rows, rows, rows, rows, P("dp", None), P(), P(("dp", "rank"), "ctx"),
            users, users, users, P(),
        ),
        out_specs=(rows, rows, rows, rows, P("dp", None), P("ctx", None)),
        check_vma=False,
    )
```

```python
import functools
import math

import jax
import jax.numpy as jnp
from jax import lax
from jax.experimental import pallas as pl
from jax.experimental.pallas import tpu as pltpu
from jax.sharding import PartitionSpec as P

F32 = jnp.float32
BF16 = jnp.bfloat16
HEADS = 8
DIM = 128
TOK = 512
HALF = 256
WIDTH = 1024
MASKED = -1e9
SCALE = 1.0 / math.sqrt(DIM)
STEP = 2
COST = 1
VMEM_LIMIT = 60 * 1024 * 1024


def dot_nt(a, b):
    return lax.dot_general(a, b, (((1,), (1,)), ((), ())), preferred_element_type=F32)


def dot_nn(a, b):
    return lax.dot_general(a, b, (((1,), (0,)), ((), ())), preferred_element_type=F32)


def dot_tn(a, b):
    return lax.dot_general(a, b, (((0,), (0,)), ((), ())), preferred_element_type=F32)


def lowest_key(meta, first, rows, axis=0):
    shape = (rows, 1) if axis == 0 else (1, rows)
    pos = first + lax.broadcasted_iota(jnp.int32, shape, axis)
    e0, e1, e2 = meta[0], meta[1], meta[2]
    start = jnp.where(pos >= e0, e0, 0)
    band = jnp.where(pos >= e0, meta[4], meta[3])
    start = jnp.where(pos >= e1, e1, start)
    band = jnp.where(pos >= e1, meta[5], band)
    start = jnp.where(pos >= e2, e2, start)
    band = jnp.where(pos >= e2, 0, band)
    return pos, jnp.maximum(start, pos - band + 1)


def mask_tile(meta, q_first, rows, k_first, cols, causal, turned=False):
    axis = 1 if turned else 0
    pos, low = lowest_key(meta, q_first, rows, axis)
    shape = (cols, rows) if turned else (rows, cols)
    key = k_first + lax.broadcasted_iota(jnp.int32, shape, 1 - axis)
    ok = key >= low
    if causal:
        ok = ok & (key <= pos)
    return jnp.where(ok, 0.0, MASKED)


def bucket_cols(row):
    count = row.shape[1]
    return jnp.transpose(jnp.broadcast_to(row.astype(F32), (DIM, count))).astype(jnp.int32)


def lanes(rows):
    return lax.broadcasted_iota(jnp.int32, (rows, DIM), 1)


def one_hot(row):
    cols = bucket_cols(row)
    return jnp.where(cols == lanes(cols.shape[0]), 1.0, 0.0).astype(BF16)


def bias_rows(table_row, cols):
    gap = jnp.abs(cols - lanes(cols.shape[0]))
    spread = jnp.broadcast_to(table_row, gap.shape)
    return jnp.take_along_axis(spread, gap, axis=1).astype(BF16)


def bias_sum(mid, cols):
    lane = lanes(cols.shape[0])
    up, down = cols + lane, cols - lane
    above = jnp.take_along_axis(mid, up & (DIM - 1), axis=1)
    below = jnp.take_along_axis(mid, down & (DIM - 1), axis=1)
    both = jnp.where(up < DIM, above, 0.0) + jnp.where((down >= 0) & (lane > 0), below, 0.0)
    return jnp.sum(both, axis=0, keepdims=True) * 0.5


def attn_of(q_aug, k_aug, mask):
    half_score = dot_nt(q_aug, k_aug) * (0.5 * SCALE) + mask
    t = jnp.tanh(half_score)
    u = 1.0 + t
    return half_score * u, t, u


def back_of(q_aug, k_aug, mask, grad, value):
    attn, t, u = attn_of(q_aug, k_aug, mask)
    slope2 = u + attn * (1.0 - t)
    score_grad2 = (dot_nt(grad, value) * slope2).astype(BF16)
    return attn.astype(BF16), score_grad2


def cat(*parts):
    return jnp.concatenate(parts, axis=1)


def each_head(tab, base=0):
    for j in range(STEP):
        h = base + pl.program_id(0) * STEP + j
        yield h, slice(j * DIM, (j + 1) * DIM), tab[pl.ds(h, 1), :]


def own_forward_body(base, meta, q, k, v, bkt, tab, *rest):
    out, mask, hot, cols = rest[-4:]

    @pl.when(pl.program_id(0) == 0)
    def _():
        mask[...] = mask_tile(meta, meta[6], TOK, meta[6], TOK, True)
        hot[...] = one_hot(bkt[...])
        cols[...] = bucket_cols(bkt[...])

    for _, at, row in each_head(tab, base):
        q_aug = cat(q[:, at], bias_rows(row, cols[...]))
        k_aug = cat(k[:, at], hot[...])
        for i in range(2):
            lo, hi = i * HALF, (i + 1) * HALF
            attn, _, _ = attn_of(q_aug[lo:hi], k_aug[:hi], mask[lo:hi, :hi])
            out[lo:hi, at] = dot_nn(attn.astype(BF16), v[:hi, at])


def norm_of(mixed):
    mixed = mixed.astype(F32)
    center = jnp.mean(mixed, axis=1, keepdims=True)
    deviation = mixed - center
    variance = jnp.mean(deviation * deviation, axis=1, keepdims=True)
    inv_std = lax.rsqrt(variance + 1e-05)
    return deviation * inv_std, inv_std


def rows_body(
    meta, q, k, v, k_bkt, bkt, tab, partial, lifted, gate,
    gate_grad, gated, mixed_grad, total, mask, hot, cols,
):
    @pl.when(pl.program_id(0) == 0)
    def _():
        mask[...] = mask_tile(meta, meta[6], TOK, meta[6] - TOK, TOK, False)
        hot[...] = one_hot(k_bkt[...])
        cols[...] = bucket_cols(bkt[...])

    for h, at, row in each_head(tab):
        q_aug = cat(q[:, at], bias_rows(row, cols[...]))
        k_aug = cat(k[:, at], hot[...])
        column = pl.ds(pl.multiple_of(h * DIM, DIM), DIM)
        for i in range(2):
            lo, hi = i * HALF, (i + 1) * HALF
            attn, _, _ = attn_of(q_aug[lo:hi], k_aug[lo:], mask[lo:hi, lo:])
            total[lo:hi, column] = (
                partial[lo:hi, at] + dot_nn(attn.astype(BF16), v[lo:, at])
            ).astype(BF16)

    @pl.when(pl.program_id(0) == HEADS // STEP - 1)
    def _():
        @pl.loop(0, TOK // 64)
        def _(c):
            for i in range(2):
                rows = pl.ds(pl.multiple_of(c * 64 + i * 32, 32), 32)
                lift = lifted[rows, :]
                gate_f = gate[rows, :].astype(F32)
                normed, inv_std = norm_of(total[rows, :])
                gate_grad[rows, :] = (lift * normed).astype(BF16)
                gated[rows, :] = (normed * gate_f).astype(BF16)
                normed_grad = lift * gate_f
                mean_one = jnp.mean(normed_grad, axis=1, keepdims=True)
                mean_two = jnp.mean(normed_grad * normed, axis=1, keepdims=True)
                mixed_grad[rows, :] = (
                    inv_std * (normed_grad - mean_one - normed * mean_two)
                ).astype(BF16)


def lifted_body(meta, cot, users, owner, weight, lifted, total):
    @pl.when(pl.program_id(0) == 0)
    def _():
        count = users.shape[0]
        slot = lax.broadcasted_iota(jnp.int32, (DIM, count), 0)
        source = lax.broadcasted_iota(jnp.int32, (DIM, count), 1)
        pick = (owner[...] == meta[7] * 3 + (slot >> 3)) & ((source & 7) == (slot & 7)) & (slot < 24)
        rows = dot_nn(jnp.where(pick, 1.0, 0.0).astype(BF16), users[...]).astype(BF16)
        pos = meta[6] + lax.broadcasted_iota(jnp.int32, (TOK, 1), 0)
        lane = lanes(TOK)
        user = lane >> 3
        last = jnp.where(user == 0, meta[0], jnp.where(user == 1, meta[1], meta[2])) - 1
        hit = (pos == last) & (lane < 24)
        for c in range(WIDTH // DIM):
            at = slice(c * DIM, (c + 1) * DIM)
            hits = jnp.where(hit & ((lane & 7) == c), 1.0, 0.0).astype(BF16)
            total[:, at] = (cot[:, at].astype(F32) + dot_nn(hits, rows)).astype(BF16)

    lifted[...] = dot_nt(total[...], weight[...])


def weight_body(meta, gated, total, keep, send):
    part = dot_tn(gated[...], total[...])
    part = part.reshape(4, 2, 32, WIDTH)

    @pl.when(meta[8] == 0)
    def _():
        keep[...] = part[:, 0].astype(BF16)
        send[...] = part[:, 1].astype(BF16)

    @pl.when(meta[8] == 1)
    def _():
        keep[...] = part[:, 1].astype(BF16)
        send[...] = part[:, 0].astype(BF16)


def own_backward_body(
    meta, q, k, v, kh, vh, kh_bkt, bkt, tab, grad,
    dq, dk, dv, bias, mask, mask_h, hot, hot_h, cols,
):
    @pl.when(pl.program_id(0) == 0)
    def _():
        mask[...] = mask_tile(meta, meta[6], TOK, meta[6], TOK, True, True)
        mask_h[...] = mask_tile(meta, meta[6], TOK, meta[6] - TOK, TOK, False)
        hot[...] = one_hot(bkt[...])
        hot_h[...] = one_hot(kh_bkt[...])
        cols[...] = bucket_cols(bkt[...])

    for h, at, row in each_head(tab):
        own_backward_head(
            q[:, at], k[:, at], v[:, at], kh[:, at], vh[:, at], row, grad[:, at],
            dq, dk, dv, bias, mask, mask_h, hot, hot_h, cols, h, at,
        )


def own_backward_head(
    q, k, v, kh, vh, row, grad, dq, dk, dv, bias, mask, mask_h, hot, hot_h, cols, h, at
):
    q_aug = cat(q, bias_rows(row, cols[...]))
    k_aug = cat(k, hot[...])
    kh_aug = cat(kh, hot_h[...])
    ge, gl = grad[:HALF], grad[HALF:]
    attn, sg = back_of(k_aug[:HALF], q_aug, mask[:HALF, :], v[:HALF], grad)
    dk[:HALF, at] = dot_nn(sg, q)
    dv[:HALF, at] = dot_nn(attn, grad)
    own = dot_tn(sg, k_aug[:HALF])
    early, late = own[:HALF], own[HALF:]
    attn, sg = back_of(k_aug[HALF:], q_aug[HALF:], mask[HALF:, HALF:], v[HALF:], gl)
    dk[HALF:, at] = dot_nn(sg, q[HALF:])
    dv[HALF:, at] = dot_nn(attn, gl)
    late = late + dot_tn(sg, k_aug[HALF:])
    _, sg = back_of(q_aug[:HALF], kh_aug, mask_h[:HALF, :], ge, vh)
    early = early + dot_nn(sg, kh_aug)
    _, sg = back_of(q_aug[HALF:], kh_aug[HALF:], mask_h[HALF:, HALF:], gl, vh[HALF:])
    late = late + dot_nn(sg, kh_aug[HALF:])
    dq[:HALF, at] = (early[:, :DIM] * (0.5 * SCALE)).astype(BF16)
    dq[HALF:, at] = (late[:, :DIM] * (0.5 * SCALE)).astype(BF16)
    bias[pl.ds(h, 1), :] = bias_sum(early[:, DIM:], cols[:HALF, :]) + bias_sum(late[:, DIM:], cols[HALF:, :])


def sent_backward_body(
    base, meta, qs, q_bkt, grad, k, v, bkt, tab, dk_own, dv_own, *rest
):
    dk, dv, mask, mask_l, hot, cols = rest[-6:]

    @pl.when(pl.program_id(0) == 0)
    def _():
        mask[...] = mask_tile(meta, meta[6] + TOK, HALF, meta[6], TOK, False, True)
        mask_l[...] = mask_tile(meta, meta[6] + TOK + HALF, HALF, meta[6] + HALF, HALF, False, True)
        hot[...] = one_hot(bkt[...])
        cols[...] = bucket_cols(q_bkt[...])

    for _, at, row in each_head(tab, base):
        added = bias_rows(row, cols[...])
        k_aug = cat(k[:, at], hot[...])
        ge, gl = grad[:HALF, at], grad[HALF:, at]
        qe, ql = qs[:HALF, at], qs[HALF:, at]
        attn, sg = back_of(k_aug, cat(qe, added[:HALF]), mask[...], v[:, at], ge)
        sum_k = dk_own[:, at] + dot_nn(sg, qe)
        sum_v = dv_own[:, at] + dot_nn(attn, ge)
        attn, sg = back_of(k_aug[HALF:], cat(ql, added[HALF:]), mask_l[...], v[HALF:, at], gl)
        dk[:HALF, at] = (sum_k[:HALF] * (0.5 * SCALE)).astype(BF16)
        dv[:HALF, at] = sum_v[:HALF].astype(BF16)
        dk[HALF:, at] = ((sum_k[HALF:] + dot_nn(sg, ql)) * (0.5 * SCALE)).astype(BF16)
        dv[HALF:, at] = (sum_v[HALF:] + dot_nn(attn, gl)).astype(BF16)


SMEM = pl.BlockSpec(memory_space=pltpu.SMEM)


def heads_of(rows, at=0):
    return pl.BlockSpec((rows, STEP * DIM), lambda h: (at, h))


def whole(*shape):
    return pl.BlockSpec(shape, lambda h: (0,) * len(shape))


def shape_of(rows, kind, cols=WIDTH):
    return jax.ShapeDtypeStruct((rows, cols), kind)


def call(body, name, grid, in_specs, out_specs, out_shape, scratch=(), aliases=None, flops=0, moved=0):
    return pl.pallas_call(
        body,
        name=name,
        grid=grid,
        in_specs=in_specs,
        out_specs=out_specs,
        out_shape=out_shape,
        scratch_shapes=list(scratch),
        input_output_aliases=aliases or {},
        cost_estimate=pl.CostEstimate(flops=flops // COST, bytes_accessed=moved // COST, transcendentals=0),
        compiler_params=pltpu.CompilerParams(vmem_limit_bytes=VMEM_LIMIT),
    )


def on_device(
    query_rows, key_rows, value_rows, gate_rows, out_grad, out_weight,
    time_bias, time_bucket, lengths, band_width, user_grad, user_owner,
):
    q, k, v = query_rows[0], key_rows[0], value_rows[0]
    gate, cot = gate_rows[0], out_grad[0]
    bkt = time_bucket
    ctx = lax.axis_index("ctx")
    rank = lax.axis_index("rank")
    n_ctx = lax.axis_size("ctx")
    n_dp = lax.axis_size("dp")
    section = lax.axis_index("dp") * lax.axis_size("rank") + rank
    ends = jnp.cumsum(lengths[0])
    first = ctx * TOK
    meta = jnp.concatenate(
        [ends, band_width[0], jnp.stack([first, section, rank])]
    ).astype(jnp.int32)
    tab = time_bias.astype(F32) * math.sqrt(DIM)
    up = [(i, i + 1) for i in range(n_ctx - 1)]
    down = [(i + 1, i) for i in range(n_ctx - 1)]

    k_came = lax.ppermute(k, "ctx", up)
    v_came = lax.ppermute(v, "ctx", up)
    q_came = lax.ppermute(q, "ctx", down)
    bkt_before = lax.ppermute(bkt, "ctx", up)
    bkt_after = lax.ppermute(bkt, "ctx", down)
    owner = jnp.pad(
        jnp.repeat(user_owner.reshape(-1, 3), 8, axis=1), ((0, 0), (0, 8)), constant_values=-1
    ).reshape(1, WIDTH)

    col = pltpu.VMEM((TOK, DIM), jnp.int32)
    hot = pltpu.VMEM((TOK, DIM), BF16)

    own_half = functools.partial(
        call, grid=(HEADS // STEP // 2,), out_shape=shape_of(TOK, F32),
        scratch=[pltpu.VMEM((TOK, TOK), F32), hot, col], flops=2_000_000_000, moved=3 << 20,
    )
    shift = HEADS // STEP // 2
    lower = pl.BlockSpec((TOK, STEP * DIM), lambda h: (0, h))
    upper = pl.BlockSpec((TOK, STEP * DIM), lambda h: (0, h + shift))
    own_out = own_half(
        functools.partial(own_forward_body, 0), "own_forward_low",
        in_specs=[SMEM, lower, lower, lower, whole(1, TOK), whole(HEADS, DIM)], out_specs=lower,
    )(meta, q, k, v, bkt, tab)

    pieces = jnp.pad(user_grad.reshape(24, DIM), ((0, 8), (0, 0)))
    half_weight = lax.dynamic_slice_in_dim(out_weight, rank * 32, 32)
    shared = jnp.concatenate([half_weight, pieces], axis=1)
    weight = lax.all_to_all(
        jnp.broadcast_to(shared[None], (2 * n_dp, 32, WIDTH + DIM)), ("dp", "rank"), 0, 0, tiled=True
    ).reshape(WIDTH, WIDTH + DIM)

    own_out = own_half(
        functools.partial(own_forward_body, HEADS // 2), "own_forward_high",
        in_specs=[SMEM, upper, upper, upper, whole(1, TOK), whole(HEADS, DIM),
                  pl.BlockSpec(memory_space=pl.ANY)],
        out_specs=upper, aliases={6: 0},
    )(meta, q, k, v, bkt, tab, own_out)

    lifted, total = call(
        lifted_body, "lifted", (4,),
        [SMEM, whole(TOK, WIDTH), pl.BlockSpec((WIDTH, DIM), lambda h: (0, WIDTH // DIM)),
         whole(1, WIDTH), pl.BlockSpec((HALF, WIDTH), lambda h: (h, 0))],
        (pl.BlockSpec((TOK, HALF), lambda h: (0, h)), whole(TOK, WIDTH)),
        (shape_of(TOK, F32), shape_of(TOK, BF16)),
        flops=1_200_000_000, moved=6 << 20,
    )(meta, cot, weight, owner, weight)

    meta_rows, q_came, bkt_after = lax.optimization_barrier((meta, q_came, bkt_after))
    gate_grad, gated, grad = call(
        rows_body, "rows", (HEADS // STEP,),
        [SMEM, heads_of(TOK), heads_of(TOK), heads_of(TOK), whole(1, TOK), whole(1, TOK),
         whole(HEADS, DIM), heads_of(TOK), whole(TOK, WIDTH), whole(TOK, WIDTH)],
        (whole(TOK, WIDTH),) * 3,
        (shape_of(TOK, BF16),) * 3,
        [pltpu.VMEM((TOK, WIDTH), BF16), pltpu.VMEM((TOK, TOK), F32), hot, col],
        flops=2_000_000_000, moved=10 << 20,
    )(meta_rows, q, k_came, v_came, bkt_before, bkt, tab, own_out, lifted, gate)
    grad_came = lax.ppermute(grad, "ctx", down)

    cut = pl.BlockSpec((TOK, HALF), lambda h: (0, h))
    piece = pl.BlockSpec((4, 32, WIDTH), lambda h: (h, 0, 0))
    keep, send = call(
        weight_body, "weight_part", (4,),
        [SMEM, cut, whole(TOK, WIDTH)],
        (piece, piece),
        (jax.ShapeDtypeStruct((16, 32, WIDTH), BF16),) * 2,
        flops=1_100_000_000, moved=6 << 20,
    )(meta, gated, total)
    other = lax.ppermute(send, "rank", [(0, 1), (1, 0)])
    pair = (keep.astype(F32) + other.astype(F32)).astype(BF16)
    rows = lax.all_to_all(pair, "dp", 0, 0, tiled=True)
    meta_own, _ = lax.optimization_barrier((meta, pair))
    passed = pl.BlockSpec(memory_space=pl.ANY)

    dq, dk_own, dv_own, bias = call(
        own_backward_body, "own_backward", (HEADS // STEP,),
        [SMEM] + [heads_of(TOK)] * 5 + [whole(1, TOK), whole(1, TOK), whole(HEADS, DIM), heads_of(TOK)],
        (heads_of(TOK), heads_of(TOK), heads_of(TOK), whole(HEADS, DIM)),
        (shape_of(TOK, BF16), shape_of(TOK, F32), shape_of(TOK, F32), shape_of(HEADS, F32, DIM)),
        [pltpu.VMEM((TOK, TOK), F32), pltpu.VMEM((TOK, TOK), F32), hot, hot, col],
        flops=10_000_000_000, moved=12 << 20,
    )(meta_own, q, k, v, k_came, v_came, bkt_before, bkt, tab, grad)

    spread = jnp.broadcast_to(bias[None, :, None], (n_dp, n_ctx, 2, DIM)).reshape(-1, DIM)
    rows, spread = lax.optimization_barrier((rows, spread))
    bias_all = lax.all_to_all(spread, ("dp", "ctx", "rank"), 0, 0, tiled=True)
    rows = jnp.sum(rows.astype(F32), axis=0)
    def sent_half(at, meta, *done):
        cols = functools.partial(pl.BlockSpec, index_map=lambda h: (0, h + at))
        out = cols((TOK, STEP * DIM))
        return call(
            functools.partial(sent_backward_body, at * STEP), "sent_backward", (HEADS // STEP // 2,),
            [SMEM, out, whole(1, TOK), out, out, out, whole(1, TOK), whole(HEADS, DIM), out, out]
            + [passed] * len(done),
            (out, out),
            (shape_of(TOK, BF16), shape_of(TOK, BF16)),
            [pltpu.VMEM((TOK, HALF), F32), pltpu.VMEM((HALF, HALF), F32), hot, col],
            aliases={10: 0, 11: 1} if done else None,
            flops=2_000_000_000, moved=5 << 20,
        )(meta, q_came, bkt_after, grad_came, k, v, bkt, tab, dk_own, dv_own, *done)

    def add_swap(rows, bit):
        return rows + lax.ppermute(rows, "ctx", [(i, i ^ bit) for i in range(n_ctx)])

    rows, meta_back = lax.optimization_barrier((rows, meta))
    done = sent_half(0, meta_back)
    rows = add_swap(rows, 4)
    rows, meta_back, *done = lax.optimization_barrier((rows, meta, *done))
    dk, dv = sent_half(HEADS // STEP // 2, meta_back, *done)
    rows = add_swap(rows, 2)
    rows, dk, dv = lax.optimization_barrier((rows, dk, dv))
    rows = add_swap(rows, 1)
    rows, bias_all = lax.optimization_barrier((rows, bias_all))
    other_rows = lax.ppermute(rows, "rank", [(0, 1), (1, 0)])
    weight_grad = jnp.concatenate(
        [jnp.where(rank == 0, rows, other_rows), jnp.where(rank == 0, other_rows, rows)], axis=0
    )
    bias_grad = jnp.sum(bias_all, axis=0, keepdims=True)
    return (dq[None], dk[None], dv[None], gate_grad[None], weight_grad, bias_grad)


def solution(mesh):
    rows = P(("dp", "rank"), "ctx", None)
    users = P(("dp", "rank"), None)
    return jax.shard_map(
        on_device,
        mesh=mesh,
        in_specs=(
            rows, rows, rows, rows, rows, P("dp", None), P(), P(("dp", "rank"), "ctx"),
            users, users, users, P(),
        ),
        out_specs=(rows, rows, rows, rows, P("dp", None), P("ctx", None)),
        check_vma=False,
    )
```
